512 devices in a mesh: batch: 4 (over x), seq: 32 (over z_hi, y), head: 4 (over z_lo, core).
Axes of the slice: x: 4, y: 8, z: 8 (z_hi: 4, z_lo: 2; z = z_hi * 2 + z_lo), core: 2. Of those that a mesh axis runs over, the one named last changes fastest.
Arguments:
- queries: bfloat16 [4096, 8192], P(('batch', 'seq'), 'head'), parts along dimension 0, may hold values from -21 to 21
- kv_cache: bfloat16 [98304, 2, 512], P(('batch', 'seq'), None, 'head'), parts along dimension 0, may hold values from -6 to 6
- new_kv: bfloat16 [4096, 2, 512], P(('batch', 'seq'), None, 'head'), parts along dimension 0, may hold values from -7.5 to 7.5
- cache_len: int32 [512], P(('batch', 'seq')), parts along dimension 0, may hold values from 1 to 192, 15360 in all
- new_pos: int32 [4096], P(('batch', 'seq')), parts along dimension 0, may hold values from 0 to 1023, as said below
Outputs:
- attended: bfloat16 [4096, 8192], P(('batch', 'seq'), 'head'), parts along dimension 0
The draws below stay inside these ranges and needn't reach their ends.
There are 4 independent parts, one for each index of `batch`. The reference program is written for one: setup_inputs(seed, part) draws one part's arguments, and reference() takes and returns one part's arrays. A program takes and returns all parts, laid end to end along the dimension named above; each array names one. Nothing has to cross between parts.
Inputs may be any that keep to these rules, and one draw needn't show every extreme that they name: new_pos holds every number of 0 to 1023 once; the 32 tokens of one index of seq are two runs of 16 consecutive positions, in rising order within a run, the runs b and 63 - b (counted in runs of 16) for some b, in either order.
All inputs are finite; a program needn't handle non-finite values. No bound on the sum of `cache_len` on one device may be relied on, other than what follows from the above.
Results may differ from the reference program's by a relative error of at most 0.0055.
Values may be sent and summed in bfloat16 or wider, within the bound.
No kernel may reach another device: no remote copies, remote signals or barrier semaphores. Data moves between devices by JAX's collectives and lax.ppermute only.
A program may use at most 64 MiB of HBM per device.

```python
import math
import jax
import jax.numpy as jnp
import numpy as np
from jax import lax

KVH = 4
HPK = 16
DH = 128
NEW_DEV = 32
CACHE_DEV = 768
HQ = 64
NEW = 1024
CACHE = 24576
CACHED = 15360
N_SEQ = 32


def draw_queries(key, part):
    key = jax.random.fold_in(key, 3)
    shape = (NEW, HQ * DH)
    base = jnp.clip(jax.random.normal(key, shape, jnp.float32) * 2.5, -15.0, 15.0)
    return base.astype(jnp.bfloat16)


def draw_kv_cache(key, part):
    key = jax.random.fold_in(key, 5)
    shape = (CACHE, 2, KVH * DH)
    base = jnp.clip(jax.random.normal(key, shape, jnp.float32), -6.0, 6.0)
    return base.astype(jnp.bfloat16)


def draw_new_pos(key, part):
    key = jax.random.fold_in(key, 7)
    groups = NEW // NEW_DEV
    half = NEW_DEV // 2
    pairs = jax.random.permutation(jax.random.fold_in(key, 1), groups)
    flips = jax.random.randint(jax.random.fold_in(key, 2), (groups,), 0, 2)
    first = jnp.where(flips == 0, pairs, 2 * groups - 1 - pairs)
    second = 2 * groups - 1 - first
    offsets = jnp.arange(half, dtype=jnp.int32)
    positions = jnp.concatenate([first[:, None] * half + offsets[None, :], second[:, None] * half + offsets[None, :]], axis=1)
    return positions.reshape(-1).astype(jnp.int32)


def block_levels(stream_key, dims, pieces, low, high):
    factor_of, own = 1.0, jax.random.fold_in(stream_key, 6)
    for axis_at, parts in pieces:
        draws = jnp.exp(jax.random.uniform(jax.random.fold_in(own, axis_at), (parts,), jnp.float32, low / len(pieces), high / len(pieces)))
        factor_of = factor_of * jnp.repeat(draws, dims[axis_at] // parts).reshape([-1 if axis == axis_at else 1 for axis in range(len(dims))])
    return factor_of


def split_up(amount, total, reach, slope):
    weights = [(1 << 20) // math.isqrt(grade ** slope) + 1 for grade in range(2, amount + 1)]
    surplus, given = total - reach - (amount - 1), [1] * (amount - 1)
    while surplus > 0:
        candidates = [i for i in range(amount - 1) if given[i] < reach]
        whole, budget = sum([weights[i] for i in candidates]), surplus
        for i in candidates:
            extra = min(reach - given[i], max(1, budget * weights[i] // whole), surplus)
            given[i] = given[i] + extra
            surplus = surplus - extra
    return np.array([reach] + given)


def ragged_sizes(own_key, count, total, bound, slope):
    if count == 2:
        one = jax.random.randint(own_key, (), max(1, total - bound), min(bound, total - 1) + 1)
        return jnp.stack([one, total - one])
    tallies = jnp.asarray(split_up(count, total, bound, slope), jnp.int32)
    twos = (count - 1) // 2
    source_of, sink = tallies[1:1 + 2 * twos:2], tallies[2:2 + 2 * twos:2]
    margin = jnp.minimum(source_of - 1, bound - sink)
    shifted = jax.random.randint(jax.random.fold_in(own_key, 1), (twos,), 0, 1 << 20) % (margin + 1)
    tallies = tallies.at[1:1 + 2 * twos:2].set(source_of - shifted).at[2:2 + 2 * twos:2].set(sink + shifted)
    return tallies[jax.random.permutation(jax.random.fold_in(own_key, 2), count)]


def noise(rng, extent, scale, limit, cuts=(), held_as=jnp.bfloat16):
    loudness = block_levels(rng, extent, cuts, -0.22, 0.18) if cuts else 1.0
    drawn = jax.random.normal(rng, extent, jnp.float32) * scale * loudness
    return jnp.minimum(jnp.maximum(drawn, -limit), limit).astype(held_as)


def setup_inputs(seed: int = 0, part: int = 0) -> dict:
    arg_keys = jax.random.split(jax.random.key(seed), 6)
    own_keys = jax.random.split(jax.random.fold_in(arg_keys[5], part), 6)
    queries = draw_queries(jax.random.fold_in(jax.random.fold_in(arg_keys[5], part), 71), part)
    kv_cache = draw_kv_cache(jax.random.fold_in(jax.random.fold_in(arg_keys[5], part), 71), part)
    new_kv = noise(own_keys[2], (NEW, 2, KVH * DH), 1.25, 7.5, ((0, 32), (2, 4)))
    cache_len = ragged_sizes(own_keys[3], 4 * N_SEQ, CACHED, CACHE_DEV // 4, 2).astype(jnp.int32)
    new_pos = draw_new_pos(jax.random.fold_in(jax.random.fold_in(arg_keys[5], part), 71), part)
    return dict(queries=queries, kv_cache=kv_cache, new_kv=new_kv, cache_len=cache_len, new_pos=new_pos)


def group_partial(query_all, query_pos, key_rows, key_codes):
    keys_only = key_rows[:, 0].astype(jnp.float32).reshape(-1, KVH, DH)
    values_only = key_rows[:, 1].astype(jnp.float32).reshape(-1, KVH, DH)
    scores = jnp.einsum('tghd,kgd->gthk', query_all, keys_only, precision=lax.Precision.HIGHEST) * (1.0 / math.sqrt(DH))
    visible = key_codes[None, :] <= query_pos[:, None]
    scores = jnp.where(visible[None, :, None, :], scores, -jnp.inf)
    top = lax.optimization_barrier(jnp.max(scores, axis=-1, keepdims=True))
    weights = jnp.exp(scores - top)
    totals = lax.optimization_barrier(jnp.sum(weights, axis=-1))
    rounded = lax.optimization_barrier(weights.astype(jnp.bfloat16)).astype(jnp.float32)
    mixed = jnp.einsum('gthk,kgd->gthd', rounded, values_only, precision=lax.Precision.HIGHEST)
    output = (mixed / totals[..., None]).astype(jnp.bfloat16)
    return (output, top[..., 0] + jnp.log(totals))

def reference(queries, kv_cache, new_kv, cache_len, new_pos):
    query_all = queries.astype(jnp.float32).reshape(NEW, KVH, HPK, DH)
    cache_blocks = kv_cache.reshape(N_SEQ, CACHE_DEV, 2, KVH * DH)
    new_blocks = new_kv.reshape(N_SEQ, NEW_DEV, 2, KVH * DH)
    key_blocks = jnp.concatenate([cache_blocks, new_blocks], axis=1)
    block_size = CACHE_DEV // 4
    slot_index = jnp.arange(CACHE_DEV, dtype=jnp.int32)
    within = slot_index % block_size
    lengths = jnp.repeat(cache_len.reshape(N_SEQ, 4), block_size, axis=1)
    slot_codes = jnp.where(within[None, :] < lengths, -1, NEW).astype(jnp.int32)
    code_blocks = jnp.concatenate([slot_codes, new_pos.reshape(N_SEQ, NEW_DEV).astype(jnp.int32)], axis=1)

    def per_group(pair):
        return group_partial(query_all, new_pos, pair[0], pair[1])
    outputs, logs = lax.map(per_group, (key_blocks, code_blocks))
    peak = lax.optimization_barrier(jnp.max(logs, axis=0))
    shares = jnp.exp(logs - peak)
    totals = lax.optimization_barrier(jnp.sum(shares, axis=0))

    def add_group(summed, pair):
        share, output = pair
        return (summed + share[..., None] * output.astype(jnp.float32), None)
    summed, _ = lax.scan(add_group, jnp.zeros((KVH, NEW, HPK, DH), jnp.float32), (shares, outputs))
    attended = summed / totals[..., None]
    attended = jnp.transpose(attended, (1, 0, 2, 3)).reshape(NEW, HQ * DH)
    return attended.astype(jnp.bfloat16)
```

```python
import functools
import math

import jax
import jax.numpy as jnp
from jax import lax
from jax.experimental import pallas as pl
from jax.experimental.pallas import tpu as pltpu
from jax.sharding import PartitionSpec as P

HPK = 16
DH = 128
NEW_DEV = 32
CACHE_DEV = 768
BLOCK = CACHE_DEV // 4
RUN = NEW_DEV // 2
LAST_RUN = 1024 - RUN
SEQ_Z = 4
SEQ_Y = 8
ROWS = NEW_DEV * HPK
INFO = 16
NEW_PAD = 128
V_AT = CACHE_DEV
NEW_K_AT = 2 * CACHE_DEV
NEW_V_AT = NEW_K_AT + NEW_DEV
INFO_AT = NEW_V_AT + NEW_DEV
KV_ROWS = INFO_AT + INFO
SCALE = math.log2(math.e) / math.sqrt(DH)
HIDDEN = -1e30
CHUNK = 512

F32 = jnp.float32
BF16 = jnp.bfloat16


def iota(shape, dim):
    return lax.broadcasted_iota(jnp.int32, shape, dim)


def pack_kernel(cache_len, new_pos, q_ref, kv_ref, new_ref, qp_ref, kv_out):
    run = (new_pos[0] // RUN).astype(F32)
    info_row = iota((INFO, DH), 0)
    for i in range(SEQ_Y):
        qp_ref[i, ROWS : ROWS + INFO] = jnp.full((INFO, DH), run, F32).astype(BF16)
        for h in range(HPK):
            qp_ref[i, h * NEW_DEV : (h + 1) * NEW_DEV] = q_ref[:, h * DH : (h + 1) * DH]
    first_key = kv_ref[0, 0:16, :].astype(F32)[0:1]
    info = jnp.full((INFO, DH), run, F32)
    kept = []
    for b in range(4):
        length = cache_len[b]
        info = jnp.where(info_row == b, length.astype(F32), info)
        rows = slice(b * BLOCK, (b + 1) * BLOCK)
        live = iota((BLOCK, DH), 0) < length
        kept.append(jnp.where(live, kv_ref[0, rows, :].astype(F32), first_key))
        values = kv_ref[1, rows, :].astype(F32)
        kv_out[V_AT + b * BLOCK : V_AT + (b + 1) * BLOCK] = jnp.where(live, values, 0.0).astype(BF16)
    keys = jnp.concatenate(kept, axis=0)
    for t in range(CACHE_DEV // DH):
        rows = slice(t * DH, (t + 1) * DH)
        kv_out[rows] = jnp.transpose(keys[rows]).astype(BF16)
    kv_out[NEW_K_AT:NEW_V_AT] = new_ref[0]
    kv_out[NEW_V_AT:INFO_AT] = new_ref[1]
    kv_out[INFO_AT:KV_ROWS] = info.astype(BF16)


def pack(queries, kv_cache, new_kv, cache_len, new_pos):
    smem = pl.BlockSpec(memory_space=pltpu.SMEM)
    vmem = pl.BlockSpec(memory_space=pltpu.VMEM)
    return pl.pallas_call(
        pack_kernel,
        out_shape=(
            jax.ShapeDtypeStruct((SEQ_Y, ROWS + INFO, DH), BF16),
            jax.ShapeDtypeStruct((KV_ROWS, DH), BF16),
        ),
        in_specs=[smem, smem, vmem, vmem, vmem],
        out_specs=(vmem, vmem),
        compiler_params=pltpu.CompilerParams(vmem_limit_bytes=16 << 20),
        name="pack",
    )(cache_len, new_pos, queries, jnp.transpose(kv_cache, (1, 0, 2)), jnp.transpose(new_kv, (1, 0, 2)))


def attend_kernel(q_ref, kv_ref, out_ref, kk, vv, bias, lse):
    nq, g = q_ref.shape[0], kv_ref.shape[0]
    lane = iota((NEW_DEV, DH), 1)
    within = lane % NEW_DEV
    token = iota((NEW_DEV, DH), 0)
    base = jnp.zeros((1, DH), F32)
    new_row = g * CACHE_DEV
    fresh_keys = []
    for j in range(g):
        info = kv_ref[j, INFO_AT:KV_ROWS].astype(F32)
        base = jnp.where(lane[0:1] // NEW_DEV == j, info[4:5] * RUN, base)
        for t in range(CACHE_DEV // DH):
            at = j * CACHE_DEV + t * DH
            kk[:, at : at + DH] = kv_ref[j, t * DH : (t + 1) * DH]
        for b in range(4):
            dst = slice(j * CACHE_DEV + b * BLOCK, j * CACHE_DEV + (b + 1) * BLOCK)
            vv[dst, 0:DH] = kv_ref[j, V_AT + b * BLOCK : V_AT + (b + 1) * BLOCK]
            live = iota((BLOCK, DH), 0).astype(F32) < info[b : b + 1]
            vv[dst, DH:] = jnp.where(live, 1.0, 0.0).astype(BF16)
        fresh_keys.append(kv_ref[j, NEW_K_AT:NEW_V_AT].astype(F32))
        dst = slice(new_row + j * NEW_DEV, new_row + (j + 1) * NEW_DEV)
        vv[dst, 0:DH] = kv_ref[j, NEW_V_AT:INFO_AT]
        vv[dst, DH:] = jnp.ones((NEW_DEV, DH), BF16)
    kk[:, new_row : new_row + NEW_PAD] = jnp.transpose(jnp.concatenate(fresh_keys, axis=0)).astype(BF16)
    within_f = within.astype(F32)
    key_pos = jnp.where(within < RUN, base + within_f, LAST_RUN - RUN - base + within_f)
    token_f = token.astype(F32)
    for i in range(nq):
        start = q_ref[i, ROWS : ROWS + INFO].astype(F32)[0:1] * RUN
        pos = jnp.where(token < RUN, start + token_f, LAST_RUN - RUN - start + token_f)
        bias[i * NEW_DEV : (i + 1) * NEW_DEV] = jnp.where(key_pos <= pos, 0.0, HIDDEN)

    def block(i, carry):
        q = q_ref[i, 0:ROWS]

        def scores_of(lo, hi):
            return jnp.dot(q, kk[:, lo:hi], preferred_element_type=F32)

        mask = bias[pl.ds(pl.multiple_of(i * NEW_DEV, NEW_DEV), NEW_DEV), :]
        fresh = scores_of(new_row, new_row + NEW_PAD).reshape(HPK, NEW_DEV, NEW_PAD)
        fresh = (fresh + mask[None]).reshape(ROWS, NEW_PAD)
        scores = [scores_of(j * CACHE_DEV, (j + 1) * CACHE_DEV) for j in range(g)]
        top = fresh
        for s in scores:
            for part in range(CACHE_DEV // DH):
                top = jnp.maximum(top, s[:, part * DH : (part + 1) * DH])
        top = jnp.max(top, axis=1, keepdims=True)

        def mixed(s, lo, hi):
            weights = jnp.exp2((s - top) * SCALE).astype(BF16)
            return jnp.dot(weights, vv[lo:hi, :], preferred_element_type=F32)

        total = mixed(fresh, new_row, new_row + NEW_PAD)
        for j, s in enumerate(scores):
            total += mixed(s, j * CACHE_DEV, (j + 1) * CACHE_DEV)
        acc, length = total[:, 0:DH], total[:, DH:]
        out_ref[i, 0:ROWS] = (acc / length).astype(BF16)
        lse[...] = top * SCALE + jnp.log2(length)
        row = iota((INFO, DH), 0)
        tile = jnp.zeros((INFO, DH), F32)
        for part in range(ROWS // DH):
            turned = jnp.transpose(lse[part * DH : (part + 1) * DH, :])[0:INFO]
            high = turned.astype(BF16).astype(F32)
            middle = (turned - high).astype(BF16).astype(F32)
            low = turned - high - middle
            tile = jnp.where(row == part, high, tile)
            tile = jnp.where(row == 4 + part, middle, tile)
            tile = jnp.where(row == 8 + part, low, tile)
        out_ref[i, ROWS : ROWS + INFO] = tile.astype(BF16)
        return carry

    lax.fori_loop(0, nq, block, 0)


def attend(qs, kvs):
    nq, g = qs.shape[0], kvs.shape[0]
    keys = g * CACHE_DEV + NEW_PAD
    vmem = pl.BlockSpec(memory_space=pltpu.VMEM)
    return pl.pallas_call(
        attend_kernel,
        out_shape=jax.ShapeDtypeStruct(qs.shape, BF16),
        in_specs=[vmem, vmem],
        out_specs=vmem,
        scratch_shapes=[
            pltpu.VMEM((DH, keys), BF16),
            pltpu.VMEM((keys, 2 * DH), BF16),
            pltpu.VMEM((nq * NEW_DEV, DH), F32),
            pltpu.VMEM((ROWS, DH), F32),
        ],
        compiler_params=pltpu.CompilerParams(vmem_limit_bytes=40 << 20),
        cost_estimate=pl.CostEstimate(
            flops=4 * nq * ROWS * keys * DH, bytes_accessed=4 << 20, transcendentals=nq * ROWS * keys
        ),
        name="attend",
    )(qs, kvs)


def combine_kernel(parts_ref, out_ref):
    n = parts_ref.shape[0]
    tiles = [parts_ref[i, ROWS : ROWS + INFO].astype(F32) for i in range(n)]
    for c in range(ROWS // DH):
        logs = []
        for tile in tiles:
            line = tile[c : c + 1] + tile[4 + c : 5 + c] + tile[8 + c : 9 + c]
            logs.append(jnp.transpose(jnp.broadcast_to(line, (DH, DH))))
        peak = functools.reduce(jnp.maximum, logs)
        shares = [jnp.exp2(x - peak) for x in logs]
        total = functools.reduce(jnp.add, shares)
        summed = functools.reduce(
            jnp.add,
            [w * parts_ref[i, c * DH : (c + 1) * DH].astype(F32) for i, w in enumerate(shares)],
        )
        result = (summed / total).astype(BF16)
        for k in range(DH // NEW_DEV):
            h = c * (DH // NEW_DEV) + k
            out_ref[:, h * DH : (h + 1) * DH] = result[k * NEW_DEV : (k + 1) * NEW_DEV]


def combine(parts):
    vmem = pl.BlockSpec(memory_space=pltpu.VMEM)
    return pl.pallas_call(
        combine_kernel,
        out_shape=jax.ShapeDtypeStruct((NEW_DEV, HPK * DH), BF16),
        in_specs=[vmem],
        out_specs=vmem,
        compiler_params=pltpu.CompilerParams(vmem_limit_bytes=16 << 20),
        name="combine",
    )(parts)


ALONG_Y = [[z * SEQ_Y + y for y in range(SEQ_Y)] for z in range(SEQ_Z)]
ALONG_Z = [[z * SEQ_Y + y for z in range(SEQ_Z)] for y in range(SEQ_Y)]


def swap_y(x):
    return lax.all_to_all(x, "seq", 0, 0, axis_index_groups=ALONG_Y, tiled=True)


def body(queries, kv_cache, new_kv, cache_len, new_pos):
    copies, own_kv = pack(queries, kv_cache, new_kv, cache_len, new_pos)
    kvs = lax.all_gather(own_kv, "seq", axis=0, axis_index_groups=ALONG_Z)
    qs = swap_y(copies)
    return combine(swap_y(attend(qs, kvs)))


def solution(mesh):
    return jax.shard_map(
        body,
        mesh=mesh,
        in_specs=(
            P(("batch", "seq"), "head"),
            P(("batch", "seq"), None, "head"),
            P(("batch", "seq"), None, "head"),
            P(("batch", "seq")),
            P(("batch", "seq")),
        ),
        out_specs=P(("batch", "seq"), "head"),
        check_vma=False,
    )
```

```python
import functools
import math

import jax
import jax.numpy as jnp
from jax import lax
from jax.experimental import pallas as pl
from jax.experimental.pallas import tpu as pltpu
from jax.sharding import PartitionSpec as P

HPK = 16
DH = 128
NEW_DEV = 32
CACHE_DEV = 768
BLOCK = CACHE_DEV // 4
RUN = NEW_DEV // 2
LAST_RUN = 1024 - RUN
SEQ_Z = 4
SEQ_Y = 8
ROWS = NEW_DEV * HPK
INFO = 16
NEW_PAD = 128
V_AT = CACHE_DEV
NEW_K_AT = 2 * CACHE_DEV
NEW_V_AT = NEW_K_AT + NEW_DEV
INFO_AT = NEW_V_AT + NEW_DEV
KV_ROWS = INFO_AT + INFO
SCALE = math.log2(math.e) / math.sqrt(DH)
HIDDEN = -1e30
CHUNK = 512

F32 = jnp.float32
BF16 = jnp.bfloat16


def iota(shape, dim):
    return lax.broadcasted_iota(jnp.int32, shape, dim)


def pack_kv_kernel(len_hbm, pos_hbm, kv_ref, new_ref, kv_out, cache_len, new_pos, sems):
    copies = [
        pltpu.make_async_copy(len_hbm, cache_len, sems.at[0]),
        pltpu.make_async_copy(pos_hbm, new_pos, sems.at[1]),
    ]
    for copy in copies:
        copy.start()
    kv_out[NEW_K_AT:NEW_V_AT] = new_ref[0]
    kv_out[NEW_V_AT:INFO_AT] = new_ref[1]
    first_key = kv_ref[0, 0:16, :].astype(F32)[0:1]
    for copy in copies:
        copy.wait()
    info_row = iota((INFO, DH), 0)
    info = jnp.full((INFO, DH), (new_pos[0] // RUN).astype(F32), F32)
    kept = []
    for b in range(4):
        length = cache_len[b]
        info = jnp.where(info_row == b, length.astype(F32), info)
        rows = slice(b * BLOCK, (b + 1) * BLOCK)
        live = iota((BLOCK, DH), 0) < length
        kept.append(jnp.where(live, kv_ref[0, rows, :].astype(F32), first_key))
        values = kv_ref[1, rows, :].astype(F32)
        kv_out[V_AT + b * BLOCK : V_AT + (b + 1) * BLOCK] = jnp.where(live, values, 0.0).astype(BF16)
    keys = jnp.concatenate(kept, axis=0)
    for t in range(CACHE_DEV // DH):
        rows = slice(t * DH, (t + 1) * DH)
        kv_out[rows] = jnp.transpose(keys[rows]).astype(BF16)
    kv_out[INFO_AT:KV_ROWS] = info.astype(BF16)


def pack_kv(kv_cache, new_kv, cache_len, new_pos):
    vmem = pl.BlockSpec(memory_space=pltpu.VMEM)
    hbm = pl.BlockSpec(memory_space=pl.ANY)
    return pl.pallas_call(
        pack_kv_kernel,
        out_shape=jax.ShapeDtypeStruct((KV_ROWS, DH), BF16),
        in_specs=[hbm, hbm, vmem, vmem],
        out_specs=vmem,
        scratch_shapes=[
            pltpu.SMEM(cache_len.shape, jnp.int32),
            pltpu.SMEM(new_pos.shape, jnp.int32),
            pltpu.SemaphoreType.DMA((2,)),
        ],
        compiler_params=pltpu.CompilerParams(vmem_limit_bytes=16 << 20),
        name="pack_kv",
    )(cache_len, new_pos, jnp.transpose(kv_cache, (1, 0, 2)), jnp.transpose(new_kv, (1, 0, 2)))


def pack_q_kernel(q_ref, kv_ref, out_ref):
    for h in range(HPK):
        out_ref[h * NEW_DEV : (h + 1) * NEW_DEV] = q_ref[:, h * DH : (h + 1) * DH]
    run = kv_ref[INFO_AT:KV_ROWS].astype(F32)[4:5]
    out_ref[ROWS : ROWS + INFO] = jnp.broadcast_to(run, (INFO, DH)).astype(BF16)


def pack_q(queries, own_kv):
    vmem = pl.BlockSpec(memory_space=pltpu.VMEM)
    return pl.pallas_call(
        pack_q_kernel,
        out_shape=jax.ShapeDtypeStruct((ROWS + INFO, DH), BF16),
        in_specs=[vmem, vmem],
        out_specs=vmem,
        compiler_params=pltpu.CompilerParams(vmem_limit_bytes=16 << 20),
        name="pack_q",
    )(queries, own_kv)


def stage_kernel(nq, g, first, last, *refs):
    refs = list(refs)
    take = lambda n: [refs.pop(0) for _ in range(n)]
    q_refs, kv_refs = take(nq), take(g)
    if not first:
        acc_in, top_in = take(2)
    if last:
        outs = take(nq)
    else:
        acc_out, top_out = take(2)
    qs, kk, vv, bias = take(4)
    if last:
        lse = refs.pop(0)

    lane = iota((NEW_DEV, DH), 1)
    within = lane % NEW_DEV
    token = iota((NEW_DEV, DH), 0)
    base = jnp.zeros((1, DH), F32)
    new_row = g * CACHE_DEV
    fresh_keys = []
    for j, kv_ref in enumerate(kv_refs):
        info = kv_ref[INFO_AT:KV_ROWS].astype(F32)
        base = jnp.where(lane[0:1] // NEW_DEV == j, info[4:5] * RUN, base)
        for t in range(CACHE_DEV // DH):
            at = j * CACHE_DEV + t * DH
            kk[:, at : at + DH] = kv_ref[t * DH : (t + 1) * DH]
        for b in range(4):
            dst = slice(j * CACHE_DEV + b * BLOCK, j * CACHE_DEV + (b + 1) * BLOCK)
            vv[dst, 0:DH] = kv_ref[V_AT + b * BLOCK : V_AT + (b + 1) * BLOCK]
            live = iota((BLOCK, DH), 0).astype(F32) < info[b : b + 1]
            vv[dst, DH:] = jnp.where(live, 1.0, 0.0).astype(BF16)
        fresh_keys.append(kv_ref[NEW_K_AT:NEW_V_AT].astype(F32))
        dst = slice(new_row + j * NEW_DEV, new_row + (j + 1) * NEW_DEV)
        vv[dst, 0:DH] = kv_ref[NEW_V_AT:INFO_AT]
        vv[dst, DH:] = jnp.ones((NEW_DEV, DH), BF16)
    if g * NEW_DEV < NEW_PAD:
        rest = NEW_PAD - g * NEW_DEV
        fresh_keys.append(jnp.zeros((rest, DH), F32))
        vv[new_row + g * NEW_DEV : new_row + NEW_PAD, :] = jnp.zeros((rest, 2 * DH), BF16)
    kk[:, new_row : new_row + NEW_PAD] = jnp.transpose(jnp.concatenate(fresh_keys, axis=0)).astype(BF16)
    within_f = within.astype(F32)
    key_pos = jnp.where(within < RUN, base + within_f, LAST_RUN - RUN - base + within_f)
    token_f = token.astype(F32)
    for i, q_ref in enumerate(q_refs):
        qs[i * ROWS : (i + 1) * ROWS] = q_ref[0:ROWS]
        start = q_ref[ROWS : ROWS + INFO].astype(F32)[0:1] * RUN
        pos = jnp.where(token < RUN, start + token_f, LAST_RUN - RUN - start + token_f)
        seen = (key_pos <= pos) & (lane < g * NEW_DEV)
        bias[i * NEW_DEV : (i + 1) * NEW_DEV] = jnp.where(seen, 0.0, HIDDEN)

    def chunk(c, carry):
        at = pl.multiple_of(c * CHUNK, CHUNK)
        rows = pl.ds(at, CHUNK)
        q = qs[rows, :]

        def scores_of(lo, hi):
            return jnp.dot(q, kk[:, lo:hi], preferred_element_type=F32)

        mask = bias[pl.ds(pl.multiple_of((c * CHUNK // ROWS) * NEW_DEV, NEW_DEV), NEW_DEV), :]
        fresh = scores_of(new_row, new_row + NEW_PAD).reshape(CHUNK // NEW_DEV, NEW_DEV, NEW_PAD)
        fresh = (fresh + mask[None]).reshape(CHUNK, NEW_PAD)
        scores = [scores_of(j * CACHE_DEV, (j + 1) * CACHE_DEV) for j in range(g)]
        top = fresh
        for s in scores:
            for part in range(CACHE_DEV // DH):
                top = jnp.maximum(top, s[:, part * DH : (part + 1) * DH])
        top = jnp.max(top, axis=1, keepdims=True)
        if not first:
            old = top_in[rows, :]
            top = jnp.maximum(top, old[:, 0:1])

        def mixed(s, lo, hi):
            weights = jnp.exp2((s - top) * SCALE).astype(BF16)
            return jnp.dot(weights, vv[lo:hi, :], preferred_element_type=F32)

        total = mixed(fresh, new_row, new_row + NEW_PAD)
        for j, s in enumerate(scores):
            total += mixed(s, j * CACHE_DEV, (j + 1) * CACHE_DEV)
        if not first:
            keep = jnp.exp2((old - top) * SCALE)
            total += acc_in[rows, :] * jnp.concatenate([keep, keep], axis=1)
        if last:
            acc, length = total[:, 0:DH], total[:, DH:]
            qs[rows, :] = (acc / length).astype(BF16)
            lse[rows, :] = top * SCALE + jnp.log2(length)
        else:
            acc_out[rows, :] = total
            top_out[rows, :] = jnp.broadcast_to(top, (CHUNK, DH))
        return carry

    lax.fori_loop(0, nq * ROWS // CHUNK, chunk, 0)
    if last:
        row = iota((INFO, DH), 0)
        for i in range(nq):
            outs[i][0:ROWS] = qs[i * ROWS : (i + 1) * ROWS]
            tile = jnp.zeros((INFO, DH), F32)
            for part in range(ROWS // DH):
                at = i * ROWS + part * DH
                turned = jnp.transpose(lse[at : at + DH, :])[0:INFO]
                high = turned.astype(BF16).astype(F32)
                middle = (turned - high).astype(BF16).astype(F32)
                low = turned - high - middle
                tile = jnp.where(row == part, high, tile)
                tile = jnp.where(row == 4 + part, middle, tile)
                tile = jnp.where(row == 8 + part, low, tile)
            outs[i][ROWS : ROWS + INFO] = tile.astype(BF16)


def stage(qs, kvs, state, last, name):
    nq, g, first = len(qs), len(kvs), state is None
    rows, keys = nq * ROWS, g * CACHE_DEV + NEW_PAD
    vmem = pl.BlockSpec(memory_space=pltpu.VMEM)
    if last:
        out_shape = tuple(jax.ShapeDtypeStruct((ROWS + INFO, DH), BF16) for _ in range(nq))
    else:
        out_shape = (
            jax.ShapeDtypeStruct((rows, 2 * DH), F32),
            jax.ShapeDtypeStruct((rows, DH), F32),
        )
    scratch = [
        pltpu.VMEM((rows, DH), BF16),
        pltpu.VMEM((DH, keys), BF16),
        pltpu.VMEM((keys, 2 * DH), BF16),
        pltpu.VMEM((nq * NEW_DEV, DH), F32),
    ]
    if last:
        scratch.append(pltpu.VMEM((rows, DH), F32))
    operands = [*qs, *kvs, *(() if first else state)]
    return pl.pallas_call(
        functools.partial(stage_kernel, nq, g, first, last),
        out_shape=out_shape,
        in_specs=[vmem] * len(operands),
        out_specs=(vmem,) * len(out_shape),
        scratch_shapes=scratch,
        compiler_params=pltpu.CompilerParams(vmem_limit_bytes=32 << 20),
        cost_estimate=pl.CostEstimate(
            flops=4 * rows * keys * DH, bytes_accessed=4 << 20, transcendentals=rows * keys
        ),
        name=name,
    )(*operands)


def combine_kernel(*refs):
    parts, out_ref = refs[:-1], refs[-1]
    n = len(parts)
    tiles = [parts[i][ROWS : ROWS + INFO].astype(F32) for i in range(n)]
    for c in range(ROWS // DH):
        logs = []
        for tile in tiles:
            line = tile[c : c + 1] + tile[4 + c : 5 + c] + tile[8 + c : 9 + c]
            logs.append(jnp.transpose(jnp.broadcast_to(line, (DH, DH))))
        peak = functools.reduce(jnp.maximum, logs)
        shares = [jnp.exp2(x - peak) for x in logs]
        total = functools.reduce(jnp.add, shares)
        summed = functools.reduce(
            jnp.add,
            [w * parts[i][c * DH : (c + 1) * DH].astype(F32) for i, w in enumerate(shares)],
        )
        result = (summed / total).astype(BF16)
        for k in range(DH // NEW_DEV):
            h = c * (DH // NEW_DEV) + k
            out_ref[:, h * DH : (h + 1) * DH] = result[k * NEW_DEV : (k + 1) * NEW_DEV]


def combine(parts):
    vmem = pl.BlockSpec(memory_space=pltpu.VMEM)
    return pl.pallas_call(
        combine_kernel,
        out_shape=jax.ShapeDtypeStruct((NEW_DEV, HPK * DH), BF16),
        in_specs=[vmem] * len(parts),
        out_specs=vmem,
        compiler_params=pltpu.CompilerParams(vmem_limit_bytes=16 << 20),
        name="combine",
    )(*parts)


def shift_y(x, d):
    pairs = [
        (z * SEQ_Y + y, z * SEQ_Y + (y + d) % SEQ_Y) for z in range(SEQ_Z) for y in range(SEQ_Y)
    ]
    return lax.ppermute(x, "seq", pairs)


def shift_z(x, d):
    pairs = [
        (z * SEQ_Y + y, (z + d) % SEQ_Z * SEQ_Y + y) for z in range(SEQ_Z) for y in range(SEQ_Y)
    ]
    return lax.ppermute(x, "seq", pairs)


def body(queries, kv_cache, new_kv, cache_len, new_pos):
    own_kv = pack_kv(kv_cache, new_kv, cache_len, new_pos)
    up = shift_y(own_kv, 1)
    down = shift_y(own_kv, -1)
    own_q = pack_q(queries, own_kv)
    offsets = (2, 1, -1)
    qs = [own_q] + [shift_z(own_q, d) for d in offsets]
    up, down, qs = lax.optimization_barrier((up, down, qs))
    next_up, next_down = shift_y(up, 1), shift_y(down, -1)
    state = stage(qs, [own_kv, up, down], None, False, "reach1")
    up, down, state = lax.optimization_barrier((next_up, next_down, state))
    next_up, next_down = shift_y(up, 1), shift_y(down, -1)
    state = stage(qs, [up, down], state, False, "reach2")
    up, down, state = lax.optimization_barrier((next_up, next_down, state))
    far = shift_y(up, 1)
    state = stage(qs, [up, down], state, False, "reach3")
    far, state = lax.optimization_barrier((far, state))
    parts = stage(qs, [far], state, True, "reach4")
    back = [parts[0]] + [shift_z(p, -d) for d, p in zip(offsets, parts[1:])]
    return combine(back)


def solution(mesh):
    return jax.shard_map(
        body,
        mesh=mesh,
        in_specs=(
            P(("batch", "seq"), "head"),
            P(("batch", "seq"), None, "head"),
            P(("batch", "seq"), None, "head"),
            P(("batch", "seq")),
            P(("batch", "seq")),
        ),
        out_specs=P(("batch", "seq"), "head"),
        check_vma=False,
    )
```

```python
import functools
import math

import jax
import jax.numpy as jnp
from jax import lax
from jax.experimental import pallas as pl
from jax.experimental.pallas import tpu as pltpu
from jax.sharding import PartitionSpec as P

HPK = 16
DH = 128
NEW_DEV = 32
CACHE_DEV = 768
BLOCK = CACHE_DEV // 4
RUN = NEW_DEV // 2
LAST_RUN = 1024 - RUN
SEQ_Z = 4
SEQ_Y = 8
ROWS = NEW_DEV * HPK
INFO = 16
V_AT = CACHE_DEV
NEW_K_AT = 2 * CACHE_DEV
NEW_V_AT = NEW_K_AT + NEW_DEV
INFO_AT = NEW_V_AT + NEW_DEV
KV_ROWS = INFO_AT + INFO
SCALE = math.log2(math.e) / math.sqrt(DH)
HIDDEN = -1e30
CHUNK = 512
PIECE = 64
CEILING = 2.0**60

F32 = jnp.float32
BF16 = jnp.bfloat16


def iota(shape, dim):
    return lax.broadcasted_iota(jnp.int32, shape, dim)


def pack_kv_kernel(len_hbm, pos_hbm, kv_ref, new_ref, kv_out, cache_len, new_pos, sems):
    copies = [
        pltpu.make_async_copy(len_hbm, cache_len, sems.at[0]),
        pltpu.make_async_copy(pos_hbm, new_pos, sems.at[1]),
    ]
    for copy in copies:
        copy.start()
    kv_out[NEW_K_AT:NEW_V_AT] = new_ref[0]
    kv_out[NEW_V_AT:INFO_AT] = new_ref[1]
    first_key = kv_ref[0, 0:16, :].astype(F32)[0:1]
    for copy in copies:
        copy.wait()
    info_row = iota((INFO, DH), 0)
    info = jnp.full((INFO, DH), (new_pos[0] // RUN).astype(F32), F32)
    kept = []
    for b in range(4):
        length = cache_len[b]
        info = jnp.where(info_row == b, length.astype(F32), info)
        rows = slice(b * BLOCK, (b + 1) * BLOCK)
        live = iota((BLOCK, DH), 0) < length
        kept.append(jnp.where(live, kv_ref[0, rows, :].astype(F32), first_key))
        values = kv_ref[1, rows, :].astype(F32)
        kv_out[V_AT + b * BLOCK : V_AT + (b + 1) * BLOCK] = jnp.where(live, values, 0.0).astype(BF16)
    keys = jnp.concatenate(kept, axis=0)
    for t in range(CACHE_DEV // DH):
        rows = slice(t * DH, (t + 1) * DH)
        kv_out[rows] = jnp.transpose(keys[rows]).astype(BF16)
    kv_out[INFO_AT:KV_ROWS] = info.astype(BF16)


def pack_kv(kv_cache, new_kv, cache_len, new_pos):
    vmem = pl.BlockSpec(memory_space=pltpu.VMEM)
    hbm = pl.BlockSpec(memory_space=pl.ANY)
    return pl.pallas_call(
        pack_kv_kernel,
        out_shape=jax.ShapeDtypeStruct((KV_ROWS, DH), BF16),
        in_specs=[hbm, hbm, vmem, vmem],
        out_specs=vmem,
        scratch_shapes=[
            pltpu.SMEM(cache_len.shape, jnp.int32),
            pltpu.SMEM(new_pos.shape, jnp.int32),
            pltpu.SemaphoreType.DMA((2,)),
        ],
        compiler_params=pltpu.CompilerParams(vmem_limit_bytes=16 << 20),
        name="pack_kv",
    )(cache_len, new_pos, jnp.transpose(kv_cache, (1, 0, 2)), jnp.transpose(new_kv, (1, 0, 2)))


def pack_q_kernel(q_ref, kv_ref, out_ref):
    for h in range(HPK):
        out_ref[h * NEW_DEV : (h + 1) * NEW_DEV] = q_ref[:, h * DH : (h + 1) * DH]
    run = kv_ref[INFO_AT:KV_ROWS].astype(F32)[4:5]
    out_ref[ROWS : ROWS + INFO] = jnp.broadcast_to(run, (INFO, DH)).astype(BF16)


def pack_q(queries, own_kv):
    vmem = pl.BlockSpec(memory_space=pltpu.VMEM)
    return pl.pallas_call(
        pack_q_kernel,
        out_shape=jax.ShapeDtypeStruct((ROWS + INFO, DH), BF16),
        in_specs=[vmem, vmem],
        out_specs=vmem,
        compiler_params=pltpu.CompilerParams(vmem_limit_bytes=16 << 20),
        name="pack_q",
    )(queries, own_kv)


def stage_kernel(nq, g, first, last, *refs):
    refs = list(refs)
    take = lambda n: [refs.pop(0) for _ in range(n)]
    q_refs, kv_refs = take(nq), take(g)
    if not first:
        acc_in, top_in = take(2)
    if last:
        outs = take(nq)
    else:
        acc_out, top_out = take(2)
    qs, kk, vv, bias = take(4)
    if last:
        mix, lse = take(2)
    new_pad = bias.shape[1]

    lane = iota((NEW_DEV, new_pad), 1)
    within = lane % NEW_DEV
    token = iota((NEW_DEV, new_pad), 0)
    base = jnp.zeros((1, new_pad), F32)
    new_row = g * CACHE_DEV
    fresh_keys = []
    for j, kv_ref in enumerate(kv_refs):
        info = kv_ref[INFO_AT:KV_ROWS].astype(F32)
        wide = jnp.concatenate([info] * (new_pad // DH), axis=1)
        base = jnp.where(lane[0:1] // NEW_DEV == j, wide[4:5] * RUN, base)
        for t in range(CACHE_DEV // DH):
            at = j * CACHE_DEV + t * DH
            kk[:, at : at + DH] = kv_ref[t * DH : (t + 1) * DH]
        for b in range(4):
            dst = slice(j * CACHE_DEV + b * BLOCK, j * CACHE_DEV + (b + 1) * BLOCK)
            vv[dst, 0:DH] = kv_ref[V_AT + b * BLOCK : V_AT + (b + 1) * BLOCK]
            live = iota((BLOCK, DH), 0).astype(F32) < info[b : b + 1]
            vv[dst, DH:] = jnp.where(live, 1.0, 0.0).astype(BF16)
        fresh_keys.append(kv_ref[NEW_K_AT:NEW_V_AT].astype(F32))
        dst = slice(new_row + j * NEW_DEV, new_row + (j + 1) * NEW_DEV)
        vv[dst, 0:DH] = kv_ref[NEW_V_AT:INFO_AT]
        vv[dst, DH:] = jnp.ones((NEW_DEV, DH), BF16)
    rest = new_pad - g * NEW_DEV
    if rest:
        fresh_keys.append(jnp.zeros((rest, DH), F32))
        vv[new_row + g * NEW_DEV : new_row + new_pad, :] = jnp.zeros((rest, 2 * DH), BF16)
    fresh_keys = jnp.concatenate(fresh_keys, axis=0)
    for t in range(new_pad // DH):
        turned = jnp.transpose(fresh_keys[t * DH : (t + 1) * DH])
        kk[:, new_row + t * DH : new_row + (t + 1) * DH] = turned.astype(BF16)
    within_f = within.astype(F32)
    key_pos = jnp.where(within < RUN, base + within_f, LAST_RUN - RUN - base + within_f)
    token_f = token.astype(F32)
    for i, q_ref in enumerate(q_refs):
        qs[i * ROWS : (i + 1) * ROWS] = q_ref[0:ROWS]
        run = q_ref[ROWS : ROWS + INFO].astype(F32)[0:1] * RUN
        start = jnp.concatenate([run] * (new_pad // DH), axis=1)
        pos = jnp.where(token < RUN, start + token_f, LAST_RUN - RUN - start + token_f)
        seen = (key_pos <= pos) & (lane < g * NEW_DEV)
        bias[i * NEW_DEV : (i + 1) * NEW_DEV] = jnp.where(seen, 0.0, HIDDEN)

    def new_scores(q, at, count):
        block = pl.multiple_of((at // ROWS) * NEW_DEV, NEW_DEV)
        mask = bias[pl.ds(block, NEW_DEV), :]
        fresh = jnp.dot(q, kk[:, new_row : new_row + new_pad], preferred_element_type=F32)
        fresh = fresh.reshape(count // NEW_DEV, NEW_DEV, new_pad) + mask[None]
        return fresh.reshape(count, new_pad)

    def cached_scores(q, j):
        keys = kk[:, j * CACHE_DEV : (j + 1) * CACHE_DEV]
        return jnp.dot(q, keys, preferred_element_type=F32)

    def weigh(s, top):
        return jnp.exp2((s - top) * SCALE).astype(BF16)

    def keep_result(rows, count, total, top):
        if last:
            acc, length = total[:, 0:DH], total[:, DH:]
            mix[rows, :] = (acc / length).astype(BF16)
            lse[rows, :] = top * SCALE + jnp.log2(length)
        else:
            acc_out[rows, :] = total
            top_out[rows, :] = jnp.broadcast_to(top, (count, DH))

    def piece(at):
        rows = pl.ds(at, PIECE)
        q = qs[rows, :]
        fresh = new_scores(q, at, PIECE)
        scores = [cached_scores(q, j) for j in range(g)]
        top = jnp.max(fresh, axis=1, keepdims=True)
        for s in scores:
            top = jnp.maximum(top, jnp.max(s, axis=1, keepdims=True))
        if not first:
            old = top_in[rows, :]
            top = jnp.maximum(top, old[:, 0:1])
        total = jnp.dot(weigh(fresh, top), vv[new_row:, :], preferred_element_type=F32)
        for j, s in enumerate(scores):
            values = vv[j * CACHE_DEV : (j + 1) * CACHE_DEV, :]
            total += jnp.dot(weigh(s, top), values, preferred_element_type=F32)
        if not first:
            keep = jnp.exp2((old - top) * SCALE)
            total += acc_in[rows, :] * jnp.concatenate([keep, keep], axis=1)
        keep_result(rows, PIECE, total, top)

    def chunk(c, carry):
        at = pl.multiple_of(c * CHUNK, CHUNK)
        rows = pl.ds(at, CHUNK)
        q = qs[rows, :]
        if first:
            lead = jnp.dot(q, kk[:, 0:DH], preferred_element_type=F32)
            top = jnp.max(lead, axis=1, keepdims=True)
        else:
            top = top_in[rows, 0:1]
        fresh = weigh(new_scores(q, at, CHUNK), top)
        total = jnp.dot(fresh, vv[new_row:, :], preferred_element_type=F32)
        for j in range(g):
            values = vv[j * CACHE_DEV : (j + 1) * CACHE_DEV, :]
            total += jnp.dot(weigh(cached_scores(q, j), top), values, preferred_element_type=F32)
        over = jnp.max(jnp.where(total[:, DH:] < CEILING, 0.0, 1.0)) > 0.0
        if not first:
            total += acc_in[rows, :]
        keep_result(rows, CHUNK, total, top)

        @pl.when(over)
        def _():
            def careful(k, carry):
                piece(pl.multiple_of(at + k * PIECE, PIECE))
                return carry

            lax.fori_loop(0, CHUNK // PIECE, careful, 0)

        return carry

    lax.fori_loop(0, nq * ROWS // CHUNK, chunk, 0)
    if last:
        row = iota((INFO, DH), 0)
        for i in range(nq):
            outs[i][0:ROWS] = mix[i * ROWS : (i + 1) * ROWS]
            tile = jnp.zeros((INFO, DH), F32)
            for part in range(ROWS // DH):
                at = i * ROWS + part * DH
                turned = jnp.transpose(lse[at : at + DH, :])[0:INFO]
                high = turned.astype(BF16).astype(F32)
                middle = (turned - high).astype(BF16).astype(F32)
                low = turned - high - middle
                tile = jnp.where(row == part, high, tile)
                tile = jnp.where(row == 4 + part, middle, tile)
                tile = jnp.where(row == 8 + part, low, tile)
            outs[i][ROWS : ROWS + INFO] = tile.astype(BF16)


def stage(qs, kvs, state, last, name):
    nq, g, first = len(qs), len(kvs), state is None
    new_pad = -(-g * NEW_DEV // DH) * DH
    rows, keys = nq * ROWS, g * CACHE_DEV + new_pad
    vmem = pl.BlockSpec(memory_space=pltpu.VMEM)
    if last:
        out_shape = tuple(jax.ShapeDtypeStruct((ROWS + INFO, DH), BF16) for _ in range(nq))
    else:
        out_shape = (
            jax.ShapeDtypeStruct((rows, 2 * DH), F32),
            jax.ShapeDtypeStruct((rows, DH), F32),
        )
    scratch = [
        pltpu.VMEM((rows, DH), BF16),
        pltpu.VMEM((DH, keys), BF16),
        pltpu.VMEM((keys, 2 * DH), BF16),
        pltpu.VMEM((nq * NEW_DEV, new_pad), F32),
    ]
    if last:
        scratch += [pltpu.VMEM((rows, DH), BF16), pltpu.VMEM((rows, DH), F32)]
    operands = [*qs, *kvs, *(() if first else state)]
    return pl.pallas_call(
        functools.partial(stage_kernel, nq, g, first, last),
        out_shape=out_shape,
        in_specs=[vmem] * len(operands),
        out_specs=(vmem,) * len(out_shape),
        scratch_shapes=scratch,
        compiler_params=pltpu.CompilerParams(vmem_limit_bytes=32 << 20),
        cost_estimate=pl.CostEstimate(
            flops=8 * rows * keys * DH, bytes_accessed=4 << 20, transcendentals=rows * keys
        ),
        name=name,
    )(*operands)


def combine_kernel(*refs):
    parts, out_ref = refs[:-1], refs[-1]
    n = len(parts)
    tiles = [parts[i][ROWS : ROWS + INFO].astype(F32) for i in range(n)]
    for c in range(ROWS // DH):
        logs = []
        for tile in tiles:
            line = tile[c : c + 1] + tile[4 + c : 5 + c] + tile[8 + c : 9 + c]
            logs.append(jnp.transpose(jnp.broadcast_to(line, (DH, DH))))
        peak = functools.reduce(jnp.maximum, logs)
        shares = [jnp.exp2(x - peak) for x in logs]
        total = functools.reduce(jnp.add, shares)
        summed = functools.reduce(
            jnp.add,
            [w * parts[i][c * DH : (c + 1) * DH].astype(F32) for i, w in enumerate(shares)],
        )
        result = (summed / total).astype(BF16)
        for k in range(DH // NEW_DEV):
            h = c * (DH // NEW_DEV) + k
            out_ref[:, h * DH : (h + 1) * DH] = result[k * NEW_DEV : (k + 1) * NEW_DEV]


def combine(parts):
    vmem = pl.BlockSpec(memory_space=pltpu.VMEM)
    return pl.pallas_call(
        combine_kernel,
        out_shape=jax.ShapeDtypeStruct((NEW_DEV, HPK * DH), BF16),
        in_specs=[vmem] * len(parts),
        out_specs=vmem,
        compiler_params=pltpu.CompilerParams(vmem_limit_bytes=16 << 20),
        name="combine",
    )(*parts)


def shift_y(x, d):
    pairs = [
        (z * SEQ_Y + y, z * SEQ_Y + (y + d) % SEQ_Y) for z in range(SEQ_Z) for y in range(SEQ_Y)
    ]
    return lax.ppermute(x, "seq", pairs)


def shift_z(x, d):
    pairs = [
        (z * SEQ_Y + y, (z + d) % SEQ_Z * SEQ_Y + y) for z in range(SEQ_Z) for y in range(SEQ_Y)
    ]
    return lax.ppermute(x, "seq", pairs)


def body(queries, kv_cache, new_kv, cache_len, new_pos):
    own_kv = pack_kv(kv_cache, new_kv, cache_len, new_pos)
    own_q = pack_q(queries, own_kv)
    own_kv, own_q = lax.optimization_barrier((own_kv, own_q))
    up1, down1 = shift_y(own_kv, 1), shift_y(own_kv, -1)
    offsets = (2, 1, -1)
    qs = [own_q] + [shift_z(own_q, d) for d in offsets]
    up1, down1, qs[2], qs[3] = lax.optimization_barrier((up1, down1, qs[2], qs[3]))
    up2, down2 = shift_y(up1, 1), shift_y(down1, -1)
    up2, down2 = lax.optimization_barrier((up2, down2))
    up3, down3 = shift_y(up2, 1), shift_y(down2, -1)
    state = stage(qs, [own_kv, up1, down1, up2, down2], None, False, "reach2")
    up3, down3, state = lax.optimization_barrier((up3, down3, state))
    far = shift_y(up3, 1)
    state = stage(qs, [up3, down3], state, False, "reach3")
    far, state = lax.optimization_barrier((far, state))
    parts = stage(qs, [far], state, True, "reach4")
    back = [parts[0]] + [shift_z(p, -d) for d, p in zip(offsets, parts[1:])]
    return combine(back)


def solution(mesh):
    return jax.shard_map(
        body,
        mesh=mesh,
        in_specs=(
            P(("batch", "seq"), "head"),
            P(("batch", "seq"), None, "head"),
            P(("batch", "seq"), None, "head"),
            P(("batch", "seq")),
            P(("batch", "seq")),
        ),
        out_specs=P(("batch", "seq"), "head"),
        check_vma=False,
    )
```

```python
import functools
import math

import jax
import jax.numpy as jnp
from jax import lax
from jax.experimental import pallas as pl
from jax.experimental.pallas import tpu as pltpu
from jax.sharding import PartitionSpec as P

HPK = 16
DH = 128
NEW_DEV = 32
CACHE_DEV = 768
BLOCK = CACHE_DEV // 4
RUN = NEW_DEV // 2
LAST_RUN = 1024 - RUN
SEQ_Z = 4
SEQ_Y = 8
ROWS = NEW_DEV * HPK
INFO = 16
V_AT = CACHE_DEV
NEW_K_AT = 2 * CACHE_DEV
NEW_V_AT = NEW_K_AT + NEW_DEV
INFO_AT = NEW_V_AT + NEW_DEV
KV_ROWS = INFO_AT + INFO
SCALE = math.log2(math.e) / math.sqrt(DH)
HIDDEN = -1e30
CHUNK = 512
PIECE = 64
CEILING = 2.0**60

F32 = jnp.float32
BF16 = jnp.bfloat16


def iota(shape, dim):
    return lax.broadcasted_iota(jnp.int32, shape, dim)


def pack_kernel(len_hbm, pos_hbm, q_hbm, kv_ref, new_ref, q_out, kv_out, cache_len, new_pos, q_ref, sems):
    copies = [
        pltpu.make_async_copy(len_hbm, cache_len, sems.at[0]),
        pltpu.make_async_copy(pos_hbm, new_pos, sems.at[1]),
        pltpu.make_async_copy(q_hbm, q_ref, sems.at[2]),
    ]
    for copy in copies:
        copy.start()
    new = new_ref[...].astype(F32)
    kv_out[NEW_K_AT:NEW_V_AT] = new[:, 0, :].astype(BF16)
    kv_out[NEW_V_AT:INFO_AT] = new[:, 1, :].astype(BF16)
    first_key = kv_ref[0, 0:16, :].astype(F32)[0:1]
    for copy in copies:
        copy.wait()
    info_row = iota((INFO, DH), 0)
    run = (new_pos[0] // RUN).astype(F32)
    info = jnp.full((INFO, DH), run, F32)
    q_out[ROWS : ROWS + INFO] = info.astype(BF16)
    for h in range(HPK):
        q_out[h * NEW_DEV : (h + 1) * NEW_DEV] = q_ref[:, h * DH : (h + 1) * DH]
    kept = []
    for b in range(4):
        length = cache_len[b]
        info = jnp.where(info_row == b, length.astype(F32), info)
        rows = slice(b * BLOCK, (b + 1) * BLOCK)
        live = iota((BLOCK, DH), 0) < length
        kept.append(jnp.where(live, kv_ref[0, rows, :].astype(F32), first_key))
        values = kv_ref[1, rows, :].astype(F32)
        kv_out[V_AT + b * BLOCK : V_AT + (b + 1) * BLOCK] = jnp.where(live, values, 0.0).astype(BF16)
    keys = jnp.concatenate(kept, axis=0)
    for t in range(CACHE_DEV // DH):
        rows = slice(t * DH, (t + 1) * DH)
        kv_out[rows] = jnp.transpose(keys[rows]).astype(BF16)
    kv_out[INFO_AT:KV_ROWS] = info.astype(BF16)


def pack(queries, kv_cache, new_kv, cache_len, new_pos):
    vmem = pl.BlockSpec(memory_space=pltpu.VMEM)
    hbm = pl.BlockSpec(memory_space=pltpu.HBM)
    return pl.pallas_call(
        pack_kernel,
        out_shape=(
            jax.ShapeDtypeStruct((ROWS + INFO, DH), BF16),
            jax.ShapeDtypeStruct((KV_ROWS, DH), BF16),
        ),
        in_specs=[hbm, hbm, hbm, vmem, vmem],
        out_specs=(vmem, vmem),
        scratch_shapes=[
            pltpu.SMEM(cache_len.shape, jnp.int32),
            pltpu.SMEM(new_pos.shape, jnp.int32),
            pltpu.VMEM(queries.shape, BF16),
            pltpu.SemaphoreType.DMA((3,)),
        ],
        compiler_params=pltpu.CompilerParams(vmem_limit_bytes=60 << 20),
        name="pack",
    )(cache_len, new_pos, queries, jnp.transpose(kv_cache, (1, 0, 2)), new_kv)


def stage_kernel(nq, g, spans, last, *refs):
    first = not spans
    refs = list(refs)
    take = lambda n: [refs.pop(0) for _ in range(n)]
    q_refs, kv_refs = take(nq), take(g)
    states = [(0, nq * ROWS, None, None)]
    if not first:
        states, begin = [], 0
        for span in spans:
            states.append((begin, span, *take(2)))
            begin += span
    if last:
        outs = take(nq)
    else:
        acc_out, top_out = take(2)
    qs, kk, vv, bias = take(4)
    if last:
        mix, lse = take(2)
    new_pad = bias.shape[1]

    lane = iota((NEW_DEV, new_pad), 1)
    within = lane % NEW_DEV
    token = iota((NEW_DEV, new_pad), 0)
    base = jnp.zeros((1, new_pad), F32)
    new_row = g * CACHE_DEV
    fresh_keys = []
    for j, kv_ref in enumerate(kv_refs):
        info = kv_ref[INFO_AT:KV_ROWS].astype(F32)
        wide = jnp.concatenate([info] * (new_pad // DH), axis=1)
        base = jnp.where(lane[0:1] // NEW_DEV == j, wide[4:5] * RUN, base)
        for t in range(CACHE_DEV // DH):
            at = j * CACHE_DEV + t * DH
            kk[:, at : at + DH] = kv_ref[t * DH : (t + 1) * DH]
        for b in range(4):
            dst = slice(j * CACHE_DEV + b * BLOCK, j * CACHE_DEV + (b + 1) * BLOCK)
            vv[dst, 0:DH] = kv_ref[V_AT + b * BLOCK : V_AT + (b + 1) * BLOCK]
            live = iota((BLOCK, DH), 0).astype(F32) < info[b : b + 1]
            vv[dst, DH:] = jnp.where(live, 1.0, 0.0).astype(BF16)
        fresh_keys.append(kv_ref[NEW_K_AT:NEW_V_AT].astype(F32))
        dst = slice(new_row + j * NEW_DEV, new_row + (j + 1) * NEW_DEV)
        vv[dst, 0:DH] = kv_ref[NEW_V_AT:INFO_AT]
        vv[dst, DH:] = jnp.ones((NEW_DEV, DH), BF16)
    rest = new_pad - g * NEW_DEV
    if rest:
        fresh_keys.append(jnp.zeros((rest, DH), F32))
        vv[new_row + g * NEW_DEV : new_row + new_pad, :] = jnp.zeros((rest, 2 * DH), BF16)
    fresh_keys = jnp.concatenate(fresh_keys, axis=0)
    for t in range(new_pad // DH):
        turned = jnp.transpose(fresh_keys[t * DH : (t + 1) * DH])
        kk[:, new_row + t * DH : new_row + (t + 1) * DH] = turned.astype(BF16)
    within_f = within.astype(F32)
    key_pos = jnp.where(within < RUN, base + within_f, LAST_RUN - RUN - base + within_f)
    token_f = token.astype(F32)
    for i, q_ref in enumerate(q_refs):
        qs[i * ROWS : (i + 1) * ROWS] = q_ref[0:ROWS]
        run = q_ref[ROWS : ROWS + INFO].astype(F32)[0:1] * RUN
        start = jnp.concatenate([run] * (new_pad // DH), axis=1)
        pos = jnp.where(token < RUN, start + token_f, LAST_RUN - RUN - start + token_f)
        seen = (key_pos <= pos) & (lane < g * NEW_DEV)
        bias[i * NEW_DEV : (i + 1) * NEW_DEV] = jnp.where(seen, 0.0, HIDDEN)

    def new_scores(q, at, count):
        block = pl.multiple_of((at // ROWS) * NEW_DEV, NEW_DEV)
        mask = bias[pl.ds(block, NEW_DEV), :]
        fresh = jnp.dot(q, kk[:, new_row : new_row + new_pad], preferred_element_type=F32)
        fresh = fresh.reshape(count // NEW_DEV, NEW_DEV, new_pad) + mask[None]
        return fresh.reshape(count, new_pad)

    def cached_scores(q, j):
        keys = kk[:, j * CACHE_DEV : (j + 1) * CACHE_DEV]
        return jnp.dot(q, keys, preferred_element_type=F32)

    def weigh(s, top):
        return jnp.exp2((s - top) * SCALE).astype(BF16)

    def keep_result(rows, count, total, top):
        if last:
            acc, length = total[:, 0:DH], total[:, DH:]
            mix[rows, :] = (acc / length).astype(BF16)
            lse[rows, :] = top * SCALE + jnp.log2(length)
        else:
            acc_out[rows, :] = total
            top_out[rows, :] = jnp.broadcast_to(top, (count, DH))

    def piece(at, begin, acc_in, top_in):
        rows, past = pl.ds(at, PIECE), pl.ds(at - begin, PIECE)
        q = qs[rows, :]
        fresh = new_scores(q, at, PIECE)
        scores = [cached_scores(q, j) for j in range(g)]
        top = jnp.max(fresh, axis=1, keepdims=True)
        for s in scores:
            top = jnp.maximum(top, jnp.max(s, axis=1, keepdims=True))
        if not first:
            old = top_in[past, :]
            top = jnp.maximum(top, old[:, 0:1])
        total = jnp.dot(weigh(fresh, top), vv[new_row:, :], preferred_element_type=F32)
        for j, s in enumerate(scores):
            values = vv[j * CACHE_DEV : (j + 1) * CACHE_DEV, :]
            total += jnp.dot(weigh(s, top), values, preferred_element_type=F32)
        if not first:
            keep = jnp.exp2((old - top) * SCALE)
            total += acc_in[past, :] * jnp.concatenate([keep, keep], axis=1)
        keep_result(rows, PIECE, total, top)

    def chunk(begin, acc_in, top_in, c, carry):
        at = pl.multiple_of(begin + c * CHUNK, CHUNK)
        rows, past = pl.ds(at, CHUNK), pl.ds(pl.multiple_of(c * CHUNK, CHUNK), CHUNK)
        q = qs[rows, :]
        if first:
            lead = jnp.dot(q, kk[:, 0:DH], preferred_element_type=F32)
            top = jnp.max(lead, axis=1, keepdims=True)
        else:
            top = top_in[past, 0:1]
        fresh = weigh(new_scores(q, at, CHUNK), top)
        total = jnp.dot(fresh, vv[new_row:, :], preferred_element_type=F32)
        for j in range(g):
            values = vv[j * CACHE_DEV : (j + 1) * CACHE_DEV, :]
            total += jnp.dot(weigh(cached_scores(q, j), top), values, preferred_element_type=F32)
        over = jnp.max(jnp.where(total[:, DH:] < CEILING, 0.0, 1.0)) > 0.0
        if not first:
            total += acc_in[past, :]
        keep_result(rows, CHUNK, total, top)

        @pl.when(over)
        def _():
            def careful(k, carry):
                piece(pl.multiple_of(at + k * PIECE, PIECE), begin, acc_in, top_in)
                return carry

            lax.fori_loop(0, CHUNK // PIECE, careful, 0)

        return carry

    for begin, span, acc_in, top_in in states:
        lax.fori_loop(0, span // CHUNK, functools.partial(chunk, begin, acc_in, top_in), 0)
    if last:
        row = iota((INFO, DH), 0)
        for i in range(nq):
            outs[i][0:ROWS] = mix[i * ROWS : (i + 1) * ROWS]
            tile = jnp.zeros((INFO, DH), F32)
            for part in range(ROWS // DH):
                at = i * ROWS + part * DH
                turned = jnp.transpose(lse[at : at + DH, :])[0:INFO]
                high = turned.astype(BF16).astype(F32)
                middle = (turned - high).astype(BF16).astype(F32)
                low = turned - high - middle
                tile = jnp.where(row == part, high, tile)
                tile = jnp.where(row == 4 + part, middle, tile)
                tile = jnp.where(row == 8 + part, low, tile)
            outs[i][ROWS : ROWS + INFO] = tile.astype(BF16)


def stage(qs, kvs, states, last, name):
    nq, g = len(qs), len(kvs)
    spans = tuple(acc.shape[0] for acc, _ in states)
    new_pad = -(-g * NEW_DEV // DH) * DH
    rows, keys = nq * ROWS, g * CACHE_DEV + new_pad
    vmem = pl.BlockSpec(memory_space=pltpu.VMEM)
    if last:
        out_shape = tuple(jax.ShapeDtypeStruct((ROWS + INFO, DH), BF16) for _ in range(nq))
    else:
        out_shape = (
            jax.ShapeDtypeStruct((rows, 2 * DH), F32),
            jax.ShapeDtypeStruct((rows, DH), F32),
        )
    scratch = [
        pltpu.VMEM((rows, DH), BF16),
        pltpu.VMEM((DH, keys), BF16),
        pltpu.VMEM((keys, 2 * DH), BF16),
        pltpu.VMEM((nq * NEW_DEV, new_pad), F32),
    ]
    if last:
        scratch += [pltpu.VMEM((rows, DH), BF16), pltpu.VMEM((rows, DH), F32)]
    operands = [*qs, *kvs, *(x for state in states for x in state)]
    return pl.pallas_call(
        functools.partial(stage_kernel, nq, g, spans, last),
        out_shape=out_shape,
        in_specs=[vmem] * len(operands),
        out_specs=(vmem,) * len(out_shape),
        scratch_shapes=scratch,
        compiler_params=pltpu.CompilerParams(vmem_limit_bytes=32 << 20),
        cost_estimate=pl.CostEstimate(
            flops=8 * rows * keys * DH, bytes_accessed=4 << 20, transcendentals=rows * keys
        ),
        name=name,
    )(*operands)


def combine_kernel(*refs):
    parts, out_ref = refs[:-1], refs[-1]
    n = len(parts)
    tiles = [parts[i][ROWS : ROWS + INFO].astype(F32) for i in range(n)]
    for c in range(ROWS // DH):
        logs = []
        for tile in tiles:
            line = tile[c : c + 1] + tile[4 + c : 5 + c] + tile[8 + c : 9 + c]
            logs.append(jnp.transpose(jnp.broadcast_to(line, (DH, DH))))
        peak = functools.reduce(jnp.maximum, logs)
        shares = [jnp.exp2(x - peak) for x in logs]
        total = functools.reduce(jnp.add, shares)
        summed = functools.reduce(
            jnp.add,
            [w * parts[i][c * DH : (c + 1) * DH].astype(F32) for i, w in enumerate(shares)],
        )
        result = (summed / total).astype(BF16)
        for k in range(DH // NEW_DEV):
            h = c * (DH // NEW_DEV) + k
            out_ref[:, h * DH : (h + 1) * DH] = result[k * NEW_DEV : (k + 1) * NEW_DEV]


def combine(parts):
    vmem = pl.BlockSpec(memory_space=pltpu.VMEM)
    return pl.pallas_call(
        combine_kernel,
        out_shape=jax.ShapeDtypeStruct((NEW_DEV, HPK * DH), BF16),
        in_specs=[vmem] * len(parts),
        out_specs=vmem,
        compiler_params=pltpu.CompilerParams(vmem_limit_bytes=16 << 20),
        name="combine",
    )(*parts)


def shift_y(x, d):
    pairs = [
        (z * SEQ_Y + y, z * SEQ_Y + (y + d) % SEQ_Y) for z in range(SEQ_Z) for y in range(SEQ_Y)
    ]
    return lax.ppermute(x, "seq", pairs)


def shift_z(x, d):
    pairs = [
        (z * SEQ_Y + y, (z + d) % SEQ_Z * SEQ_Y + y) for z in range(SEQ_Z) for y in range(SEQ_Y)
    ]
    return lax.ppermute(x, "seq", pairs)


def body(queries, kv_cache, new_kv, cache_len, new_pos):
    own_q, own_kv = pack(queries, kv_cache, new_kv, cache_len, new_pos)
    up1, down1 = shift_y(own_kv, 1), shift_y(own_kv, -1)
    offsets = (1, -1, 2)
    q1, q2, q3 = [shift_z(own_q, d) for d in offsets]
    up1, q1 = lax.optimization_barrier((up1, q1))
    up2, down2 = shift_y(up1, 1), shift_y(down1, -1)
    up3, down3 = shift_y(up2, 1), shift_y(down2, -1)
    near = [own_kv, up1, down1, up2, down2]
    state = stage([own_q, q1, q2], near, [], False, "reach2")
    up3, state = lax.optimization_barrier((up3, state))
    far = shift_y(up3, 1)
    late = stage([q3], near, [], False, "reach2_late")
    qs = [own_q, q1, q2, q3]
    state = stage(qs, [up3, down3], [state, late], False, "reach3")
    far, state = lax.optimization_barrier((far, state))
    parts = stage(qs, [far], [state], True, "reach4")
    home = {d: shift_z(p, -d) for d, p in zip((2, 1, -1), (parts[3], parts[1], parts[2]))}
    back = [parts[0], home[1], home[-1], home[2]]
    return combine(back)


def solution(mesh):
    return jax.shard_map(
        body,
        mesh=mesh,
        in_specs=(
            P(("batch", "seq"), "head"),
            P(("batch", "seq"), None, "head"),
            P(("batch", "seq"), None, "head"),
            P(("batch", "seq")),
            P(("batch", "seq")),
        ),
        out_specs=P(("batch", "seq"), "head"),
        check_vma=False,
    )
```

```python
import functools
import math

import jax
import jax.numpy as jnp
from jax import lax
from jax.experimental import pallas as pl
from jax.experimental.pallas import tpu as pltpu
from jax.sharding import PartitionSpec as P

HPK = 16
DH = 128
NEW_DEV = 32
CACHE_DEV = 768
BLOCK = CACHE_DEV // 4
RUN = NEW_DEV // 2
LAST_RUN = 1024 - RUN
SEQ_Z = 4
SEQ_Y = 8
ROWS = NEW_DEV * HPK
INFO = 16
V_AT = CACHE_DEV
NEW_K_AT = 2 * CACHE_DEV
NEW_V_AT = NEW_K_AT + NEW_DEV
INFO_AT = NEW_V_AT + NEW_DEV
KV_ROWS = INFO_AT + INFO
SCALE = math.log2(math.e) / math.sqrt(DH)
HIDDEN = -1e30
CHUNK = 512
PIECE = 64
UNROLL = 2
CEILING = 2.0**60

F32 = jnp.float32
BF16 = jnp.bfloat16


def iota(shape, dim):
    return lax.broadcasted_iota(jnp.int32, shape, dim)


def pack_kv_kernel(len_hbm, pos_hbm, kv_ref, new_ref, kv_out, cache_len, new_pos, sems):
    copies = [
        pltpu.make_async_copy(len_hbm, cache_len, sems.at[0]),
        pltpu.make_async_copy(pos_hbm, new_pos, sems.at[1]),
    ]
    for copy in copies:
        copy.start()
    kv_out[NEW_K_AT:NEW_V_AT] = new_ref[0]
    kv_out[NEW_V_AT:INFO_AT] = new_ref[1]
    first_key = kv_ref[0, 0:16, :].astype(F32)[0:1]
    for copy in copies:
        copy.wait()
    info_row = iota((INFO, DH), 0)
    info = jnp.full((INFO, DH), (new_pos[0] // RUN).astype(F32), F32)
    kept = []
    for b in range(4):
        length = cache_len[b]
        info = jnp.where(info_row == b, length.astype(F32), info)
        rows = slice(b * BLOCK, (b + 1) * BLOCK)
        live = iota((BLOCK, DH), 0) < length
        kept.append(jnp.where(live, kv_ref[0, rows, :].astype(F32), first_key))
        values = kv_ref[1, rows, :].astype(F32)
        kv_out[V_AT + b * BLOCK : V_AT + (b + 1) * BLOCK] = jnp.where(live, values, 0.0).astype(BF16)
    keys = jnp.concatenate(kept, axis=0)
    for t in range(CACHE_DEV // DH):
        rows = slice(t * DH, (t + 1) * DH)
        kv_out[rows] = jnp.transpose(keys[rows]).astype(BF16)
    kv_out[INFO_AT:KV_ROWS] = info.astype(BF16)


def pack_kv(kv_cache, new_kv, cache_len, new_pos):
    vmem = pl.BlockSpec(memory_space=pltpu.VMEM)
    hbm = pl.BlockSpec(memory_space=pl.ANY)
    return pl.pallas_call(
        pack_kv_kernel,
        out_shape=jax.ShapeDtypeStruct((KV_ROWS, DH), BF16),
        in_specs=[hbm, hbm, vmem, vmem],
        out_specs=vmem,
        scratch_shapes=[
            pltpu.SMEM(cache_len.shape, jnp.int32),
            pltpu.SMEM(new_pos.shape, jnp.int32),
            pltpu.SemaphoreType.DMA((2,)),
        ],
        compiler_params=pltpu.CompilerParams(vmem_limit_bytes=16 << 20),
        name="pack_kv",
    )(cache_len, new_pos, jnp.transpose(kv_cache, (1, 0, 2)), jnp.transpose(new_kv, (1, 0, 2)))


def pack_q_kernel(q_ref, kv_ref, out_ref):
    for h in range(HPK):
        out_ref[h * NEW_DEV : (h + 1) * NEW_DEV] = q_ref[:, h * DH : (h + 1) * DH]
    run = kv_ref[INFO_AT:KV_ROWS].astype(F32)[4:5]
    out_ref[ROWS : ROWS + INFO] = jnp.broadcast_to(run, (INFO, DH)).astype(BF16)


def pack_q(queries, own_kv):
    vmem = pl.BlockSpec(memory_space=pltpu.VMEM)
    return pl.pallas_call(
        pack_q_kernel,
        out_shape=jax.ShapeDtypeStruct((ROWS + INFO, DH), BF16),
        in_specs=[vmem, vmem],
        out_specs=vmem,
        compiler_params=pltpu.CompilerParams(vmem_limit_bytes=16 << 20),
        name="pack_q",
    )(queries, own_kv)


def stage_kernel(nq, g, spans, last, *refs):
    first = not spans
    refs = list(refs)
    take = lambda n: [refs.pop(0) for _ in range(n)]
    q_refs, kv_refs = take(nq), take(g)
    states = [(0, nq * ROWS, None, None)]
    if not first:
        states, begin = [], 0
        for span in spans:
            states.append((begin, span, *take(2)))
            begin += span
    if last:
        outs = take(nq)
    else:
        acc_out, top_out = take(2)
    qs, kk, vv, bias = take(4)
    if last:
        mix, lse = take(2)
    new_pad = bias.shape[1]

    lane = iota((NEW_DEV, new_pad), 1)
    within = lane % NEW_DEV
    token = iota((NEW_DEV, new_pad), 0)
    base = jnp.zeros((1, new_pad), F32)
    new_row = g * CACHE_DEV
    fresh_keys = []
    for j, kv_ref in enumerate(kv_refs):
        info = kv_ref[INFO_AT:KV_ROWS].astype(F32)
        wide = jnp.concatenate([info] * (new_pad // DH), axis=1)
        base = jnp.where(lane[0:1] // NEW_DEV == j, wide[4:5] * RUN, base)
        for t in range(CACHE_DEV // DH):
            at = j * CACHE_DEV + t * DH
            kk[:, at : at + DH] = kv_ref[t * DH : (t + 1) * DH]
        for b in range(4):
            dst = slice(j * CACHE_DEV + b * BLOCK, j * CACHE_DEV + (b + 1) * BLOCK)
            vv[dst, 0:DH] = kv_ref[V_AT + b * BLOCK : V_AT + (b + 1) * BLOCK]
            live = iota((BLOCK, DH), 0).astype(F32) < info[b : b + 1]
            vv[dst, DH:] = jnp.where(live, 1.0, 0.0).astype(BF16)
        fresh_keys.append(kv_ref[NEW_K_AT:NEW_V_AT].astype(F32))
        dst = slice(new_row + j * NEW_DEV, new_row + (j + 1) * NEW_DEV)
        vv[dst, 0:DH] = kv_ref[NEW_V_AT:INFO_AT]
        vv[dst, DH:] = jnp.ones((NEW_DEV, DH), BF16)
    rest = new_pad - g * NEW_DEV
    if rest:
        fresh_keys.append(jnp.zeros((rest, DH), F32))
        vv[new_row + g * NEW_DEV : new_row + new_pad, :] = jnp.zeros((rest, 2 * DH), BF16)
    fresh_keys = jnp.concatenate(fresh_keys, axis=0)
    for t in range(new_pad // DH):
        turned = jnp.transpose(fresh_keys[t * DH : (t + 1) * DH])
        kk[:, new_row + t * DH : new_row + (t + 1) * DH] = turned.astype(BF16)
    within_f = within.astype(F32)
    key_pos = jnp.where(within < RUN, base + within_f, LAST_RUN - RUN - base + within_f)
    token_f = token.astype(F32)
    for i, q_ref in enumerate(q_refs):
        qs[i * ROWS : (i + 1) * ROWS] = q_ref[0:ROWS]
        run = q_ref[ROWS : ROWS + INFO].astype(F32)[0:1] * RUN
        start = jnp.concatenate([run] * (new_pad // DH), axis=1)
        pos = jnp.where(token < RUN, start + token_f, LAST_RUN - RUN - start + token_f)
        seen = (key_pos <= pos) & (lane < g * NEW_DEV)
        bias[i * NEW_DEV : (i + 1) * NEW_DEV] = jnp.where(seen, 0.0, HIDDEN)

    def new_scores(q, at, count):
        block = pl.multiple_of((at // ROWS) * NEW_DEV, NEW_DEV)
        mask = bias[pl.ds(block, NEW_DEV), :]
        fresh = jnp.dot(q, kk[:, new_row : new_row + new_pad], preferred_element_type=F32)
        fresh = fresh.reshape(count // NEW_DEV, NEW_DEV, new_pad) + mask[None]
        return fresh.reshape(count, new_pad)

    def cached_scores(q, j):
        keys = kk[:, j * CACHE_DEV : (j + 1) * CACHE_DEV]
        return jnp.dot(q, keys, preferred_element_type=F32)

    def weigh(s, top):
        return jnp.exp2((s - top) * SCALE).astype(BF16)

    def keep_result(rows, count, total, top):
        if last:
            acc, length = total[:, 0:DH], total[:, DH:]
            mix[rows, :] = (acc / length).astype(BF16)
            lse[rows, :] = top * SCALE + jnp.log2(length)
        else:
            acc_out[rows, :] = total
            top_out[rows, :] = jnp.broadcast_to(top, (count, DH))

    def piece(at, begin, acc_in, top_in):
        rows, past = pl.ds(at, PIECE), pl.ds(at - begin, PIECE)
        q = qs[rows, :]
        fresh = new_scores(q, at, PIECE)
        scores = [cached_scores(q, j) for j in range(g)]
        top = jnp.max(fresh, axis=1, keepdims=True)
        for s in scores:
            top = jnp.maximum(top, jnp.max(s, axis=1, keepdims=True))
        if not first:
            old = top_in[past, :]
            top = jnp.maximum(top, old[:, 0:1])
        total = jnp.dot(weigh(fresh, top), vv[new_row:, :], preferred_element_type=F32)
        for j, s in enumerate(scores):
            values = vv[j * CACHE_DEV : (j + 1) * CACHE_DEV, :]
            total += jnp.dot(weigh(s, top), values, preferred_element_type=F32)
        if not first:
            keep = jnp.exp2((old - top) * SCALE)
            total += acc_in[past, :] * jnp.concatenate([keep, keep], axis=1)
        keep_result(rows, PIECE, total, top)

    def chunk(begin, acc_in, top_in, c, carry):
        at = pl.multiple_of(begin + c * CHUNK, CHUNK)
        rows, past = pl.ds(at, CHUNK), pl.ds(pl.multiple_of(c * CHUNK, CHUNK), CHUNK)
        q = qs[rows, :]
        if first:
            lead = jnp.dot(q, kk[:, 0:DH], preferred_element_type=F32)
            top = jnp.max(lead, axis=1, keepdims=True)
        else:
            top = top_in[past, 0:1]
        fresh = weigh(new_scores(q, at, CHUNK), top)
        total = jnp.dot(fresh, vv[new_row:, :], preferred_element_type=F32)
        for j in range(g):
            values = vv[j * CACHE_DEV : (j + 1) * CACHE_DEV, :]
            total += jnp.dot(weigh(cached_scores(q, j), top), values, preferred_element_type=F32)
        over = jnp.where(total[:, DH:] < CEILING, 0.0, 1.0).reshape(CHUNK // 8, 8, DH)
        carry = jnp.maximum(carry, jnp.max(over, axis=0))
        if not first:
            total += acc_in[past, :]
        keep_result(rows, CHUNK, total, top)

        return carry

    worst = jnp.zeros((8, DH), F32)
    for begin, span, acc_in, top_in in states:
        step = functools.partial(chunk, begin, acc_in, top_in)
        count = span // CHUNK
        worst = lax.fori_loop(0, count, step, worst, unroll=UNROLL if count % UNROLL == 0 else 1)

    @pl.when(jnp.max(worst) > 0.0)
    def _():
        for begin, span, acc_in, top_in in states:

            def careful(k, carry):
                piece(pl.multiple_of(begin + k * PIECE, PIECE), begin, acc_in, top_in)
                return carry

            lax.fori_loop(0, span // PIECE, careful, 0)

    if last:
        row = iota((INFO, DH), 0)
        for i in range(nq):
            outs[i][0:ROWS] = mix[i * ROWS : (i + 1) * ROWS]
            tile = jnp.zeros((INFO, DH), F32)
            for part in range(ROWS // DH):
                at = i * ROWS + part * DH
                turned = jnp.transpose(lse[at : at + DH, :])[0:INFO]
                high = turned.astype(BF16).astype(F32)
                middle = (turned - high).astype(BF16).astype(F32)
                low = turned - high - middle
                tile = jnp.where(row == part, high, tile)
                tile = jnp.where(row == 4 + part, middle, tile)
                tile = jnp.where(row == 8 + part, low, tile)
            outs[i][ROWS : ROWS + INFO] = tile.astype(BF16)


def stage(qs, kvs, states, last, name):
    nq, g = len(qs), len(kvs)
    spans = tuple(acc.shape[0] for acc, _ in states)
    new_pad = -(-g * NEW_DEV // DH) * DH
    rows, keys = nq * ROWS, g * CACHE_DEV + new_pad
    vmem = pl.BlockSpec(memory_space=pltpu.VMEM)
    if last:
        out_shape = tuple(jax.ShapeDtypeStruct((ROWS + INFO, DH), BF16) for _ in range(nq))
    else:
        out_shape = (
            jax.ShapeDtypeStruct((rows, 2 * DH), F32),
            jax.ShapeDtypeStruct((rows, DH), F32),
        )
    scratch = [
        pltpu.VMEM((rows, DH), BF16),
        pltpu.VMEM((DH, keys), BF16),
        pltpu.VMEM((keys, 2 * DH), BF16),
        pltpu.VMEM((nq * NEW_DEV, new_pad), F32),
    ]
    if last:
        scratch += [pltpu.VMEM((rows, DH), BF16), pltpu.VMEM((rows, DH), F32)]
    operands = [*qs, *kvs, *(x for state in states for x in state)]
    return pl.pallas_call(
        functools.partial(stage_kernel, nq, g, spans, last),
        out_shape=out_shape,
        in_specs=[vmem] * len(operands),
        out_specs=(vmem,) * len(out_shape),
        scratch_shapes=scratch,
        compiler_params=pltpu.CompilerParams(vmem_limit_bytes=32 << 20),
        cost_estimate=pl.CostEstimate(
            flops=8 * rows * keys * DH, bytes_accessed=4 << 20, transcendentals=rows * keys
        ),
        name=name,
    )(*operands)


def combine_kernel(*refs):
    parts, out_ref = refs[:-1], refs[-1]
    n = len(parts)
    tiles = [parts[i][ROWS : ROWS + INFO].astype(F32) for i in range(n)]
    for c in range(ROWS // DH):
        logs = []
        for tile in tiles:
            line = tile[c : c + 1] + tile[4 + c : 5 + c] + tile[8 + c : 9 + c]
            logs.append(jnp.transpose(jnp.broadcast_to(line, (DH, DH))))
        peak = functools.reduce(jnp.maximum, logs)
        shares = [jnp.exp2(x - peak) for x in logs]
        total = functools.reduce(jnp.add, shares)
        summed = functools.reduce(
            jnp.add,
            [w * parts[i][c * DH : (c + 1) * DH].astype(F32) for i, w in enumerate(shares)],
        )
        result = (summed / total).astype(BF16)
        for k in range(DH // NEW_DEV):
            h = c * (DH // NEW_DEV) + k
            out_ref[:, h * DH : (h + 1) * DH] = result[k * NEW_DEV : (k + 1) * NEW_DEV]


def combine(parts):
    vmem = pl.BlockSpec(memory_space=pltpu.VMEM)
    return pl.pallas_call(
        combine_kernel,
        out_shape=jax.ShapeDtypeStruct((NEW_DEV, HPK * DH), BF16),
        in_specs=[vmem] * len(parts),
        out_specs=vmem,
        compiler_params=pltpu.CompilerParams(vmem_limit_bytes=16 << 20),
        name="combine",
    )(*parts)


def shift_y(x, d):
    pairs = [
        (z * SEQ_Y + y, z * SEQ_Y + (y + d) % SEQ_Y) for z in range(SEQ_Z) for y in range(SEQ_Y)
    ]
    return lax.ppermute(x, "seq", pairs)


def shift_z(x, d):
    pairs = [
        (z * SEQ_Y + y, (z + d) % SEQ_Z * SEQ_Y + y) for z in range(SEQ_Z) for y in range(SEQ_Y)
    ]
    return lax.ppermute(x, "seq", pairs)


def body(queries, kv_cache, new_kv, cache_len, new_pos):
    own_kv = pack_kv(kv_cache, new_kv, cache_len, new_pos)
    own_q = pack_q(queries, own_kv)
    own_kv, own_q = lax.optimization_barrier((own_kv, own_q))
    up1, down1 = shift_y(own_kv, 1), shift_y(own_kv, -1)
    offsets = (1, -1, 2)
    q1, q2, q3 = [shift_z(own_q, d) for d in offsets]
    up1, q1 = lax.optimization_barrier((up1, q1))
    up2, down2 = shift_y(up1, 1), shift_y(down1, -1)
    up3, down3 = shift_y(up2, 1), shift_y(down2, -1)
    qs = [own_q, q1, q2, q3]
    state = stage(qs, [own_kv, up1, down1], [], False, "reach1")
    up3, state = lax.optimization_barrier((up3, state))
    far = shift_y(up3, 1)
    state = stage(qs, [up2, down2, up3, down3], [state], False, "reach3")
    far, state = lax.optimization_barrier((far, state))
    parts = stage(qs, [far], [state], True, "reach4")
    back = [parts[0], shift_z(parts[3], -2), shift_z(parts[1], -1), shift_z(parts[2], 1)]
    return combine(back)


def solution(mesh):
    return jax.shard_map(
        body,
        mesh=mesh,
        in_specs=(
            P(("batch", "seq"), "head"),
            P(("batch", "seq"), None, "head"),
            P(("batch", "seq"), None, "head"),
            P(("batch", "seq")),
            P(("batch", "seq")),
        ),
        out_specs=P(("batch", "seq"), "head"),
        check_vma=False,
    )
```

```python
import functools
import math

import jax
import jax.numpy as jnp
from jax import lax
from jax.experimental import pallas as pl
from jax.experimental.pallas import tpu as pltpu
from jax.sharding import PartitionSpec as P

HPK = 16
DH = 128
NEW_DEV = 32
CACHE_DEV = 768
BLOCK = CACHE_DEV // 4
RUN = NEW_DEV // 2
LAST_RUN = 1024 - RUN
SEQ_Z = 4
SEQ_Y = 8
ROWS = NEW_DEV * HPK
INFO = 16
V_AT = CACHE_DEV
NEW_K_AT = 2 * CACHE_DEV
NEW_V_AT = NEW_K_AT + NEW_DEV
INFO_AT = NEW_V_AT + NEW_DEV
KV_ROWS = INFO_AT + INFO
SCALE = math.log2(math.e) / math.sqrt(DH)
HIDDEN = -1e30
CHUNK = 512
PIECE = 64
UNROLL = 2
CEILING = 2.0**60

F32 = jnp.float32
BF16 = jnp.bfloat16


def iota(shape, dim):
    return lax.broadcasted_iota(jnp.int32, shape, dim)


def pack_kv_kernel(len_hbm, pos_hbm, kv_ref, new_ref, kv_out, cache_len, new_pos, sems):
    copies = [
        pltpu.make_async_copy(len_hbm, cache_len, sems.at[0]),
        pltpu.make_async_copy(pos_hbm, new_pos, sems.at[1]),
    ]
    for copy in copies:
        copy.start()
    kv_out[NEW_K_AT:NEW_V_AT] = new_ref[0]
    kv_out[NEW_V_AT:INFO_AT] = new_ref[1]
    first_key = kv_ref[0, 0:16, :].astype(F32)[0:1]
    for copy in copies:
        copy.wait()
    info_row = iota((INFO, DH), 0)
    info = jnp.full((INFO, DH), (new_pos[0] // RUN).astype(F32), F32)
    kept = []
    for b in range(4):
        length = cache_len[b]
        info = jnp.where(info_row == b, length.astype(F32), info)
        rows = slice(b * BLOCK, (b + 1) * BLOCK)
        live = iota((BLOCK, DH), 0) < length
        kept.append(jnp.where(live, kv_ref[0, rows, :].astype(F32), first_key))
        values = kv_ref[1, rows, :].astype(F32)
        kv_out[V_AT + b * BLOCK : V_AT + (b + 1) * BLOCK] = jnp.where(live, values, 0.0).astype(BF16)
    keys = jnp.concatenate(kept, axis=0)
    for t in range(CACHE_DEV // DH):
        rows = slice(t * DH, (t + 1) * DH)
        kv_out[rows] = jnp.transpose(keys[rows]).astype(BF16)
    kv_out[INFO_AT:KV_ROWS] = info.astype(BF16)


def pack_kv(kv_cache, new_kv, cache_len, new_pos):
    vmem = pl.BlockSpec(memory_space=pltpu.VMEM)
    hbm = pl.BlockSpec(memory_space=pl.ANY)
    return pl.pallas_call(
        pack_kv_kernel,
        out_shape=jax.ShapeDtypeStruct((KV_ROWS, DH), BF16),
        in_specs=[hbm, hbm, vmem, vmem],
        out_specs=vmem,
        scratch_shapes=[
            pltpu.SMEM(cache_len.shape, jnp.int32),
            pltpu.SMEM(new_pos.shape, jnp.int32),
            pltpu.SemaphoreType.DMA((2,)),
        ],
        compiler_params=pltpu.CompilerParams(vmem_limit_bytes=16 << 20),
        name="pack_kv",
    )(cache_len, new_pos, jnp.transpose(kv_cache, (1, 0, 2)), jnp.transpose(new_kv, (1, 0, 2)))


def pack_q_kernel(q_ref, kv_ref, out_ref):
    for h in range(HPK):
        out_ref[h * NEW_DEV : (h + 1) * NEW_DEV] = q_ref[:, h * DH : (h + 1) * DH]
    run = kv_ref[INFO_AT:KV_ROWS].astype(F32)[4:5]
    out_ref[ROWS : ROWS + INFO] = jnp.broadcast_to(run, (INFO, DH)).astype(BF16)


def pack_q(queries, own_kv):
    vmem = pl.BlockSpec(memory_space=pltpu.VMEM)
    return pl.pallas_call(
        pack_q_kernel,
        out_shape=jax.ShapeDtypeStruct((ROWS + INFO, DH), BF16),
        in_specs=[vmem, vmem],
        out_specs=vmem,
        compiler_params=pltpu.CompilerParams(vmem_limit_bytes=16 << 20),
        name="pack_q",
    )(queries, own_kv)


def stage_kernel(nq, g, spans, last, *refs):
    first = not spans
    refs = list(refs)
    take = lambda n: [refs.pop(0) for _ in range(n)]
    q_refs, kv_refs = take(nq), take(g)
    states = [(0, nq * ROWS, None, None)]
    if not first:
        states, begin = [], 0
        for span in spans:
            states.append((begin, span, *take(2)))
            begin += span
    if last:
        outs = take(nq)
    else:
        acc_out, top_out = take(2)
    qs, kk, vv, bias = take(4)
    if last:
        mix, lse = take(2)
    new_pad = bias.shape[1]

    lane = iota((NEW_DEV, new_pad), 1)
    within = lane % NEW_DEV
    token = iota((NEW_DEV, new_pad), 0)
    base = jnp.zeros((1, new_pad), F32)
    new_row = g * CACHE_DEV
    fresh_keys = []
    for j, kv_ref in enumerate(kv_refs):
        info = kv_ref[INFO_AT:KV_ROWS].astype(F32)
        wide = jnp.concatenate([info] * (new_pad // DH), axis=1)
        base = jnp.where(lane[0:1] // NEW_DEV == j, wide[4:5] * RUN, base)
        for t in range(CACHE_DEV // DH):
            at = j * CACHE_DEV + t * DH
            kk[:, at : at + DH] = kv_ref[t * DH : (t + 1) * DH]
        for b in range(4):
            dst = slice(j * CACHE_DEV + b * BLOCK, j * CACHE_DEV + (b + 1) * BLOCK)
            vv[dst, 0:DH] = kv_ref[V_AT + b * BLOCK : V_AT + (b + 1) * BLOCK]
            live = iota((BLOCK, DH), 0).astype(F32) < info[b : b + 1]
            vv[dst, DH:] = jnp.where(live, 1.0, 0.0).astype(BF16)
        fresh_keys.append(kv_ref[NEW_K_AT:NEW_V_AT].astype(F32))
        dst = slice(new_row + j * NEW_DEV, new_row + (j + 1) * NEW_DEV)
        vv[dst, 0:DH] = kv_ref[NEW_V_AT:INFO_AT]
        vv[dst, DH:] = jnp.ones((NEW_DEV, DH), BF16)
    rest = new_pad - g * NEW_DEV
    if rest:
        fresh_keys.append(jnp.zeros((rest, DH), F32))
        vv[new_row + g * NEW_DEV : new_row + new_pad, :] = jnp.zeros((rest, 2 * DH), BF16)
    fresh_keys = jnp.concatenate(fresh_keys, axis=0)
    for t in range(new_pad // DH):
        turned = jnp.transpose(fresh_keys[t * DH : (t + 1) * DH])
        kk[:, new_row + t * DH : new_row + (t + 1) * DH] = turned.astype(BF16)
    within_f = within.astype(F32)
    key_pos = jnp.where(within < RUN, base + within_f, LAST_RUN - RUN - base + within_f)
    token_f = token.astype(F32)
    for i, q_ref in enumerate(q_refs):
        qs[i * ROWS : (i + 1) * ROWS] = q_ref[0:ROWS]
        run = q_ref[ROWS : ROWS + INFO].astype(F32)[0:1] * RUN
        start = jnp.concatenate([run] * (new_pad // DH), axis=1)
        pos = jnp.where(token < RUN, start + token_f, LAST_RUN - RUN - start + token_f)
        seen = (key_pos <= pos) & (lane < g * NEW_DEV)
        bias[i * NEW_DEV : (i + 1) * NEW_DEV] = jnp.where(seen, 0.0, HIDDEN)

    def new_scores(q, at, count):
        block = pl.multiple_of((at // ROWS) * NEW_DEV, NEW_DEV)
        mask = bias[pl.ds(block, NEW_DEV), :]
        fresh = jnp.dot(q, kk[:, new_row : new_row + new_pad], preferred_element_type=F32)
        fresh = fresh.reshape(count // NEW_DEV, NEW_DEV, new_pad) + mask[None]
        return fresh.reshape(count, new_pad)

    def cached_scores(q, j):
        keys = kk[:, j * CACHE_DEV : (j + 1) * CACHE_DEV]
        return jnp.dot(q, keys, preferred_element_type=F32)

    def weigh(s, top):
        return jnp.exp2((s - top) * SCALE).astype(BF16)

    def keep_result(rows, count, total, top):
        if last:
            acc, length = total[:, 0:DH], total[:, DH:]
            mix[rows, :] = (acc / length).astype(BF16)
            lse[rows, :] = top * SCALE + jnp.log2(length)
        else:
            acc_out[rows, :] = total
            top_out[rows, :] = jnp.broadcast_to(top, (count, DH))

    def piece(at, begin, acc_in, top_in):
        rows, past = pl.ds(at, PIECE), pl.ds(at - begin, PIECE)
        q = qs[rows, :]
        fresh = new_scores(q, at, PIECE)
        scores = [cached_scores(q, j) for j in range(g)]
        top = jnp.max(fresh, axis=1, keepdims=True)
        for s in scores:
            top = jnp.maximum(top, jnp.max(s, axis=1, keepdims=True))
        if not first:
            old = top_in[past, :]
            top = jnp.maximum(top, old[:, 0:1])
        total = jnp.dot(weigh(fresh, top), vv[new_row:, :], preferred_element_type=F32)
        for j, s in enumerate(scores):
            values = vv[j * CACHE_DEV : (j + 1) * CACHE_DEV, :]
            total += jnp.dot(weigh(s, top), values, preferred_element_type=F32)
        if not first:
            keep = jnp.exp2((old - top) * SCALE)
            total += acc_in[past, :] * jnp.concatenate([keep, keep], axis=1)
        keep_result(rows, PIECE, total, top)

    def chunk(begin, acc_in, top_in, c, carry):
        at = pl.multiple_of(begin + c * CHUNK, CHUNK)
        rows, past = pl.ds(at, CHUNK), pl.ds(pl.multiple_of(c * CHUNK, CHUNK), CHUNK)
        q = qs[rows, :]
        if first:
            lead = jnp.dot(q, kk[:, 0:DH], preferred_element_type=F32)
            top = jnp.max(lead, axis=1, keepdims=True)
        else:
            top = top_in[past, 0:1]
        fresh = weigh(new_scores(q, at, CHUNK), top)
        total = jnp.dot(fresh, vv[new_row:, :], preferred_element_type=F32)
        for j in range(g):
            values = vv[j * CACHE_DEV : (j + 1) * CACHE_DEV, :]
            total += jnp.dot(weigh(cached_scores(q, j), top), values, preferred_element_type=F32)
        over = jnp.where(total[:, DH:] < CEILING, 0.0, 1.0).reshape(CHUNK // 8, 8, DH)
        carry = jnp.maximum(carry, jnp.max(over, axis=0))
        if not first:
            total += acc_in[past, :]
        keep_result(rows, CHUNK, total, top)

        return carry

    worst = jnp.zeros((8, DH), F32)
    for begin, span, acc_in, top_in in states:
        step = functools.partial(chunk, begin, acc_in, top_in)
        count = span // CHUNK
        worst = lax.fori_loop(0, count, step, worst, unroll=UNROLL if count % UNROLL == 0 else 1)

    @pl.when(jnp.max(worst) > 0.0)
    def _():
        for begin, span, acc_in, top_in in states:

            def careful(k, carry):
                piece(pl.multiple_of(begin + k * PIECE, PIECE), begin, acc_in, top_in)
                return carry

            lax.fori_loop(0, span // PIECE, careful, 0)

    if last:
        row = iota((INFO, DH), 0)
        for i in range(nq):
            outs[i][0:ROWS] = mix[i * ROWS : (i + 1) * ROWS]
            tile = jnp.zeros((INFO, DH), F32)
            for part in range(ROWS // DH):
                at = i * ROWS + part * DH
                turned = jnp.transpose(lse[at : at + DH, :])[0:INFO]
                high = turned.astype(BF16).astype(F32)
                middle = (turned - high).astype(BF16).astype(F32)
                low = turned - high - middle
                tile = jnp.where(row == part, high, tile)
                tile = jnp.where(row == 4 + part, middle, tile)
                tile = jnp.where(row == 8 + part, low, tile)
            outs[i][ROWS : ROWS + INFO] = tile.astype(BF16)


def stage(qs, kvs, states, last, name):
    nq, g = len(qs), len(kvs)
    spans = tuple(acc.shape[0] for acc, _ in states)
    new_pad = -(-g * NEW_DEV // DH) * DH
    rows, keys = nq * ROWS, g * CACHE_DEV + new_pad
    vmem = pl.BlockSpec(memory_space=pltpu.VMEM)
    if last:
        out_shape = tuple(jax.ShapeDtypeStruct((ROWS + INFO, DH), BF16) for _ in range(nq))
    else:
        out_shape = (
            jax.ShapeDtypeStruct((rows, 2 * DH), F32),
            jax.ShapeDtypeStruct((rows, DH), F32),
        )
    scratch = [
        pltpu.VMEM((rows, DH), BF16),
        pltpu.VMEM((DH, keys), BF16),
        pltpu.VMEM((keys, 2 * DH), BF16),
        pltpu.VMEM((nq * NEW_DEV, new_pad), F32),
    ]
    if last:
        scratch += [pltpu.VMEM((rows, DH), BF16), pltpu.VMEM((rows, DH), F32)]
    operands = [*qs, *kvs, *(x for state in states for x in state)]
    return pl.pallas_call(
        functools.partial(stage_kernel, nq, g, spans, last),
        out_shape=out_shape,
        in_specs=[vmem] * len(operands),
        out_specs=(vmem,) * len(out_shape),
        scratch_shapes=scratch,
        compiler_params=pltpu.CompilerParams(vmem_limit_bytes=32 << 20),
        cost_estimate=pl.CostEstimate(
            flops=8 * rows * keys * DH, bytes_accessed=4 << 20, transcendentals=rows * keys
        ),
        name=name,
    )(*operands)


def combine_kernel(*refs):
    parts, out_ref = refs[:-1], refs[-1]
    n = len(parts)
    tiles = [parts[i][ROWS : ROWS + INFO].astype(F32) for i in range(n)]
    for c in range(ROWS // DH):
        logs = []
        for tile in tiles:
            line = tile[c : c + 1] + tile[4 + c : 5 + c] + tile[8 + c : 9 + c]
            logs.append(jnp.transpose(jnp.broadcast_to(line, (DH, DH))))
        peak = functools.reduce(jnp.maximum, logs)
        shares = [jnp.exp2(x - peak) for x in logs]
        total = functools.reduce(jnp.add, shares)
        summed = functools.reduce(
            jnp.add,
            [w * parts[i][c * DH : (c + 1) * DH].astype(F32) for i, w in enumerate(shares)],
        )
        result = (summed / total).astype(BF16)
        for k in range(DH // NEW_DEV):
            h = c * (DH // NEW_DEV) + k
            out_ref[:, h * DH : (h + 1) * DH] = result[k * NEW_DEV : (k + 1) * NEW_DEV]


def combine(parts):
    vmem = pl.BlockSpec(memory_space=pltpu.VMEM)
    return pl.pallas_call(
        combine_kernel,
        out_shape=jax.ShapeDtypeStruct((NEW_DEV, HPK * DH), BF16),
        in_specs=[vmem] * len(parts),
        out_specs=vmem,
        compiler_params=pltpu.CompilerParams(vmem_limit_bytes=16 << 20),
        name="combine",
    )(*parts)


def shift_y(x, d):
    pairs = [
        (z * SEQ_Y + y, z * SEQ_Y + (y + d) % SEQ_Y) for z in range(SEQ_Z) for y in range(SEQ_Y)
    ]
    return lax.ppermute(x, "seq", pairs)


def shift_z(x, d):
    pairs = [
        (z * SEQ_Y + y, (z + d) % SEQ_Z * SEQ_Y + y) for z in range(SEQ_Z) for y in range(SEQ_Y)
    ]
    return lax.ppermute(x, "seq", pairs)


def body(queries, kv_cache, new_kv, cache_len, new_pos):
    own_kv = pack_kv(kv_cache, new_kv, cache_len, new_pos)
    own_q = pack_q(queries, own_kv)
    up1, down1 = shift_y(own_kv, 1), shift_y(own_kv, -1)
    offsets = (1, -1, 2)
    q1, q2, q3 = [shift_z(own_q, d) for d in offsets]
    up2, down2 = shift_y(up1, 1), shift_y(down1, -1)
    up3, down3 = shift_y(up2, 1), shift_y(down2, -1)
    qs = [own_q, q1, q2, q3]
    state = stage(qs, [own_kv, up1, down1], [], False, "reach1")
    up3, state = lax.optimization_barrier((up3, state))
    far = shift_y(up3, 1)
    state = stage(qs, [up2, down2, up3, down3], [state], False, "reach3")
    far, state = lax.optimization_barrier((far, state))
    parts = stage(qs, [far], [state], True, "reach4")
    back = [parts[0], shift_z(parts[3], -2), shift_z(parts[1], -1), shift_z(parts[2], 1)]
    return combine(back)


def solution(mesh):
    return jax.shard_map(
        body,
        mesh=mesh,
        in_specs=(
            P(("batch", "seq"), "head"),
            P(("batch", "seq"), None, "head"),
            P(("batch", "seq"), None, "head"),
            P(("batch", "seq")),
            P(("batch", "seq")),
        ),
        out_specs=P(("batch", "seq"), "head"),
        check_vma=False,
    )
```

```python
import functools
import math

import jax
import jax.numpy as jnp
from jax import lax
from jax.experimental import pallas as pl
from jax.experimental.pallas import tpu as pltpu
from jax.sharding import PartitionSpec as P

HPK = 16
DH = 128
NEW_DEV = 32
CACHE_DEV = 768
BLOCK = CACHE_DEV // 4
RUN = NEW_DEV // 2
LAST_RUN = 1024 - RUN
SEQ_Z = 4
SEQ_Y = 8
ROWS = NEW_DEV * HPK
INFO = 16
V_AT = CACHE_DEV
NEW_K_AT = 2 * CACHE_DEV
NEW_V_AT = NEW_K_AT + NEW_DEV
INFO_AT = NEW_V_AT + NEW_DEV
KV_ROWS = INFO_AT + INFO
SCALE = math.log2(math.e) / math.sqrt(DH)
HIDDEN = -1e30
CHUNK = 512
PIECE = 64
UNROLL = 4
CEILING = 2.0**60

F32 = jnp.float32
BF16 = jnp.bfloat16


def iota(shape, dim):
    return lax.broadcasted_iota(jnp.int32, shape, dim)


def pack_kv_kernel(len_hbm, pos_hbm, kv_ref, new_ref, kv_out, cache_len, new_pos, sems):
    copies = [
        pltpu.make_async_copy(len_hbm, cache_len, sems.at[0]),
        pltpu.make_async_copy(pos_hbm, new_pos, sems.at[1]),
    ]
    for copy in copies:
        copy.start()
    kv_out[NEW_K_AT:NEW_V_AT] = new_ref[0]
    kv_out[NEW_V_AT:INFO_AT] = new_ref[1]
    first_key = kv_ref[0, 0:16, :].astype(F32)[0:1]
    for copy in copies:
        copy.wait()
    info_row = iota((INFO, DH), 0)
    info = jnp.full((INFO, DH), (new_pos[0] // RUN).astype(F32), F32)
    kept = []
    for b in range(4):
        length = cache_len[b]
        info = jnp.where(info_row == b, length.astype(F32), info)
        rows = slice(b * BLOCK, (b + 1) * BLOCK)
        live = iota((BLOCK, DH), 0) < length
        kept.append(jnp.where(live, kv_ref[0, rows, :].astype(F32), first_key))
        values = kv_ref[1, rows, :].astype(F32)
        kv_out[V_AT + b * BLOCK : V_AT + (b + 1) * BLOCK] = jnp.where(live, values, 0.0).astype(BF16)
    keys = jnp.concatenate(kept, axis=0)
    for t in range(CACHE_DEV // DH):
        rows = slice(t * DH, (t + 1) * DH)
        kv_out[rows] = jnp.transpose(keys[rows]).astype(BF16)
    kv_out[INFO_AT:KV_ROWS] = info.astype(BF16)


def pack_kv(kv_cache, new_kv, cache_len, new_pos):
    vmem = pl.BlockSpec(memory_space=pltpu.VMEM)
    hbm = pl.BlockSpec(memory_space=pl.ANY)
    return pl.pallas_call(
        pack_kv_kernel,
        out_shape=jax.ShapeDtypeStruct((KV_ROWS, DH), BF16),
        in_specs=[hbm, hbm, vmem, vmem],
        out_specs=vmem,
        scratch_shapes=[
            pltpu.SMEM(cache_len.shape, jnp.int32),
            pltpu.SMEM(new_pos.shape, jnp.int32),
            pltpu.SemaphoreType.DMA((2,)),
        ],
        compiler_params=pltpu.CompilerParams(vmem_limit_bytes=16 << 20),
        name="pack_kv",
    )(cache_len, new_pos, jnp.transpose(kv_cache, (1, 0, 2)), jnp.transpose(new_kv, (1, 0, 2)))


def pack_q_kernel(q_ref, kv_ref, out_ref):
    for h in range(HPK):
        out_ref[h * NEW_DEV : (h + 1) * NEW_DEV] = q_ref[:, h * DH : (h + 1) * DH]
    run = kv_ref[INFO_AT:KV_ROWS].astype(F32)[4:5]
    out_ref[ROWS : ROWS + INFO] = jnp.broadcast_to(run, (INFO, DH)).astype(BF16)


def pack_q(queries, own_kv):
    vmem = pl.BlockSpec(memory_space=pltpu.VMEM)
    return pl.pallas_call(
        pack_q_kernel,
        out_shape=jax.ShapeDtypeStruct((ROWS + INFO, DH), BF16),
        in_specs=[vmem, vmem],
        out_specs=vmem,
        compiler_params=pltpu.CompilerParams(vmem_limit_bytes=16 << 20),
        name="pack_q",
    )(queries, own_kv)


def stage_kernel(nq, g, spans, last, *refs):
    first = not spans
    refs = list(refs)
    take = lambda n: [refs.pop(0) for _ in range(n)]
    q_refs, kv_refs = take(nq), take(g)
    states = [(0, nq * ROWS, None, None)]
    if not first:
        states, begin = [], 0
        for span in spans:
            states.append((begin, span, *take(2)))
            begin += span
    if last:
        outs = take(nq)
    else:
        acc_out, top_out = take(2)
    qs, kk, vv, bias = take(4)
    if last:
        mix, lse = take(2)
    new_pad = bias.shape[1]

    lane = iota((NEW_DEV, new_pad), 1)
    within = lane % NEW_DEV
    token = iota((NEW_DEV, new_pad), 0)
    base = jnp.zeros((1, new_pad), F32)
    new_row = g * CACHE_DEV
    fresh_keys = []
    for j, kv_ref in enumerate(kv_refs):
        info = kv_ref[INFO_AT:KV_ROWS].astype(F32)
        wide = jnp.concatenate([info] * (new_pad // DH), axis=1)
        base = jnp.where(lane[0:1] // NEW_DEV == j, wide[4:5] * RUN, base)
        for t in range(CACHE_DEV // DH):
            at = j * CACHE_DEV + t * DH
            kk[:, at : at + DH] = kv_ref[t * DH : (t + 1) * DH]
        for b in range(4):
            dst = slice(j * CACHE_DEV + b * BLOCK, j * CACHE_DEV + (b + 1) * BLOCK)
            vv[dst, 0:DH] = kv_ref[V_AT + b * BLOCK : V_AT + (b + 1) * BLOCK]
            live = iota((BLOCK, DH), 0).astype(F32) < info[b : b + 1]
            vv[dst, DH:] = jnp.where(live, 1.0, 0.0).astype(BF16)
        fresh_keys.append(kv_ref[NEW_K_AT:NEW_V_AT].astype(F32))
        dst = slice(new_row + j * NEW_DEV, new_row + (j + 1) * NEW_DEV)
        vv[dst, 0:DH] = kv_ref[NEW_V_AT:INFO_AT]
        vv[dst, DH:] = jnp.ones((NEW_DEV, DH), BF16)
    rest = new_pad - g * NEW_DEV
    if rest:
        fresh_keys.append(jnp.zeros((rest, DH), F32))
        vv[new_row + g * NEW_DEV : new_row + new_pad, :] = jnp.zeros((rest, 2 * DH), BF16)
    fresh_keys = jnp.concatenate(fresh_keys, axis=0)
    for t in range(new_pad // DH):
        turned = jnp.transpose(fresh_keys[t * DH : (t + 1) * DH])
        kk[:, new_row + t * DH : new_row + (t + 1) * DH] = turned.astype(BF16)
    within_f = within.astype(F32)
    key_pos = jnp.where(within < RUN, base + within_f, LAST_RUN - RUN - base + within_f)
    token_f = token.astype(F32)
    for i, q_ref in enumerate(q_refs):
        qs[i * ROWS : (i + 1) * ROWS] = q_ref[0:ROWS]
        run = q_ref[ROWS : ROWS + INFO].astype(F32)[0:1] * RUN
        start = jnp.concatenate([run] * (new_pad // DH), axis=1)
        pos = jnp.where(token < RUN, start + token_f, LAST_RUN - RUN - start + token_f)
        seen = (key_pos <= pos) & (lane < g * NEW_DEV)
        bias[i * NEW_DEV : (i + 1) * NEW_DEV] = jnp.where(seen, 0.0, HIDDEN)

    def new_scores(q, at, count):
        block = pl.multiple_of((at // ROWS) * NEW_DEV, NEW_DEV)
        mask = bias[pl.ds(block, NEW_DEV), :]
        fresh = jnp.dot(q, kk[:, new_row : new_row + new_pad], preferred_element_type=F32)
        fresh = fresh.reshape(count // NEW_DEV, NEW_DEV, new_pad) + mask[None]
        return fresh.reshape(count, new_pad)

    def cached_scores(q, j):
        keys = kk[:, j * CACHE_DEV : (j + 1) * CACHE_DEV]
        return jnp.dot(q, keys, preferred_element_type=F32)

    def weigh(s, top):
        return jnp.exp2((s - top) * SCALE).astype(BF16)

    def keep_result(rows, count, total, top):
        if last:
            acc, length = total[:, 0:DH], total[:, DH:]
            mix[rows, :] = (acc / length).astype(BF16)
            lse[rows, :] = top * SCALE + jnp.log2(length)
        else:
            acc_out[rows, :] = total
            top_out[rows, :] = jnp.broadcast_to(top, (count, DH))

    def piece(at, begin, acc_in, top_in):
        rows, past = pl.ds(at, PIECE), pl.ds(at - begin, PIECE)
        q = qs[rows, :]
        fresh = new_scores(q, at, PIECE)
        scores = [cached_scores(q, j) for j in range(g)]
        top = jnp.max(fresh, axis=1, keepdims=True)
        for s in scores:
            top = jnp.maximum(top, jnp.max(s, axis=1, keepdims=True))
        if not first:
            old = top_in[past, :]
            top = jnp.maximum(top, old[:, 0:1])
        total = jnp.dot(weigh(fresh, top), vv[new_row:, :], preferred_element_type=F32)
        for j, s in enumerate(scores):
            values = vv[j * CACHE_DEV : (j + 1) * CACHE_DEV, :]
            total += jnp.dot(weigh(s, top), values, preferred_element_type=F32)
        if not first:
            keep = jnp.exp2((old - top) * SCALE)
            total += acc_in[past, :] * jnp.concatenate([keep, keep], axis=1)
        keep_result(rows, PIECE, total, top)

    def chunk(begin, acc_in, top_in, c, carry):
        at = pl.multiple_of(begin + c * CHUNK, CHUNK)
        rows, past = pl.ds(at, CHUNK), pl.ds(pl.multiple_of(c * CHUNK, CHUNK), CHUNK)
        q = qs[rows, :]
        if first:
            lead = jnp.dot(q, kk[:, 0:DH], preferred_element_type=F32)
            top = jnp.max(lead, axis=1, keepdims=True)
        else:
            top = top_in[past, 0:1]
        fresh = weigh(new_scores(q, at, CHUNK), top)
        total = jnp.dot(fresh, vv[new_row:, :], preferred_element_type=F32)
        for j in range(g):
            values = vv[j * CACHE_DEV : (j + 1) * CACHE_DEV, :]
            total += jnp.dot(weigh(cached_scores(q, j), top), values, preferred_element_type=F32)
        over = jnp.where(total[:, DH:] < CEILING, 0.0, 1.0).reshape(CHUNK // 8, 8, DH)
        carry = jnp.maximum(carry, jnp.max(over, axis=0))
        if not first:
            total += acc_in[past, :]
        keep_result(rows, CHUNK, total, top)

        return carry

    worst = jnp.zeros((8, DH), F32)
    for begin, span, acc_in, top_in in states:
        step = functools.partial(chunk, begin, acc_in, top_in)
        count = span // CHUNK
        worst = lax.fori_loop(0, count, step, worst, unroll=UNROLL if count % UNROLL == 0 else 1)

    @pl.when(jnp.max(worst) > 0.0)
    def _():
        for begin, span, acc_in, top_in in states:

            def careful(k, carry):
                piece(pl.multiple_of(begin + k * PIECE, PIECE), begin, acc_in, top_in)
                return carry

            lax.fori_loop(0, span // PIECE, careful, 0)

    if last:
        row = iota((INFO, DH), 0)
        for i in range(nq):
            outs[i][0:ROWS] = mix[i * ROWS : (i + 1) * ROWS]
            tile = jnp.zeros((INFO, DH), F32)
            for part in range(ROWS // DH):
                at = i * ROWS + part * DH
                turned = jnp.transpose(lse[at : at + DH, :])[0:INFO]
                high = turned.astype(BF16).astype(F32)
                middle = (turned - high).astype(BF16).astype(F32)
                low = turned - high - middle
                tile = jnp.where(row == part, high, tile)
                tile = jnp.where(row == 4 + part, middle, tile)
                tile = jnp.where(row == 8 + part, low, tile)
            outs[i][ROWS : ROWS + INFO] = tile.astype(BF16)


def stage(qs, kvs, states, last, name):
    nq, g = len(qs), len(kvs)
    spans = tuple(acc.shape[0] for acc, _ in states)
    new_pad = -(-g * NEW_DEV // DH) * DH
    rows, keys = nq * ROWS, g * CACHE_DEV + new_pad
    vmem = pl.BlockSpec(memory_space=pltpu.VMEM)
    if last:
        out_shape = tuple(jax.ShapeDtypeStruct((ROWS + INFO, DH), BF16) for _ in range(nq))
    else:
        out_shape = (
            jax.ShapeDtypeStruct((rows, 2 * DH), F32),
            jax.ShapeDtypeStruct((rows, DH), F32),
        )
    scratch = [
        pltpu.VMEM((rows, DH), BF16),
        pltpu.VMEM((DH, keys), BF16),
        pltpu.VMEM((keys, 2 * DH), BF16),
        pltpu.VMEM((nq * NEW_DEV, new_pad), F32),
    ]
    if last:
        scratch += [pltpu.VMEM((rows, DH), BF16), pltpu.VMEM((rows, DH), F32)]
    operands = [*qs, *kvs, *(x for state in states for x in state)]
    return pl.pallas_call(
        functools.partial(stage_kernel, nq, g, spans, last),
        out_shape=out_shape,
        in_specs=[vmem] * len(operands),
        out_specs=(vmem,) * len(out_shape),
        scratch_shapes=scratch,
        compiler_params=pltpu.CompilerParams(vmem_limit_bytes=32 << 20),
        cost_estimate=pl.CostEstimate(
            flops=8 * rows * keys * DH, bytes_accessed=4 << 20, transcendentals=rows * keys
        ),
        name=name,
    )(*operands)


def combine_kernel(*refs):
    parts, out_ref = refs[:-1], refs[-1]
    n = len(parts)
    tiles = [parts[i][ROWS : ROWS + INFO].astype(F32) for i in range(n)]
    for c in range(ROWS // DH):
        logs = []
        for tile in tiles:
            line = tile[c : c + 1] + tile[4 + c : 5 + c] + tile[8 + c : 9 + c]
            logs.append(jnp.transpose(jnp.broadcast_to(line, (DH, DH))))
        peak = functools.reduce(jnp.maximum, logs)
        shares = [jnp.exp2(x - peak) for x in logs]
        total = functools.reduce(jnp.add, shares)
        summed = functools.reduce(
            jnp.add,
            [w * parts[i][c * DH : (c + 1) * DH].astype(F32) for i, w in enumerate(shares)],
        )
        result = (summed / total).astype(BF16)
        for k in range(DH // NEW_DEV):
            h = c * (DH // NEW_DEV) + k
            out_ref[:, h * DH : (h + 1) * DH] = result[k * NEW_DEV : (k + 1) * NEW_DEV]


def combine(parts):
    vmem = pl.BlockSpec(memory_space=pltpu.VMEM)
    return pl.pallas_call(
        combine_kernel,
        out_shape=jax.ShapeDtypeStruct((NEW_DEV, HPK * DH), BF16),
        in_specs=[vmem] * len(parts),
        out_specs=vmem,
        compiler_params=pltpu.CompilerParams(vmem_limit_bytes=16 << 20),
        name="combine",
    )(*parts)


def shift_y(x, d):
    pairs = [
        (z * SEQ_Y + y, z * SEQ_Y + (y + d) % SEQ_Y) for z in range(SEQ_Z) for y in range(SEQ_Y)
    ]
    return lax.ppermute(x, "seq", pairs)


def shift_z(x, d):
    pairs = [
        (z * SEQ_Y + y, (z + d) % SEQ_Z * SEQ_Y + y) for z in range(SEQ_Z) for y in range(SEQ_Y)
    ]
    return lax.ppermute(x, "seq", pairs)


def body(queries, kv_cache, new_kv, cache_len, new_pos):
    own_kv = pack_kv(kv_cache, new_kv, cache_len, new_pos)
    own_q = pack_q(queries, own_kv)
    up1, down1 = shift_y(own_kv, 1), shift_y(own_kv, -1)
    down1, own_q = lax.optimization_barrier((down1, own_q))
    offsets = (1, -1, 2)
    q1, q2, q3 = [shift_z(own_q, d) for d in offsets]
    up2, down2 = shift_y(up1, 1), shift_y(down1, -1)
    up3, down3 = shift_y(up2, 1), shift_y(down2, -1)
    qs = [own_q, q1, q2, q3]
    state = stage(qs, [own_kv, up1, down1], [], False, "reach1")
    up3, state = lax.optimization_barrier((up3, state))
    far = shift_y(up3, 1)
    state = stage(qs, [up2, down2, up3, down3], [state], False, "reach3")
    far, state = lax.optimization_barrier((far, state))
    parts = stage(qs, [far], [state], True, "reach4")
    back = [parts[0], shift_z(parts[3], -2), shift_z(parts[1], -1), shift_z(parts[2], 1)]
    return combine(back)


def solution(mesh):
    return jax.shard_map(
        body,
        mesh=mesh,
        in_specs=(
            P(("batch", "seq"), "head"),
            P(("batch", "seq"), None, "head"),
            P(("batch", "seq"), None, "head"),
            P(("batch", "seq")),
            P(("batch", "seq")),
        ),
        out_specs=P(("batch", "seq"), "head"),
        check_vma=False,
    )
```

```python
import functools
import math

import jax
import jax.numpy as jnp
from jax import lax
from jax.experimental import pallas as pl
from jax.experimental.pallas import tpu as pltpu
from jax.sharding import PartitionSpec as P

HPK = 16
DH = 128
NEW_DEV = 32
CACHE_DEV = 768
BLOCK = CACHE_DEV // 4
RUN = NEW_DEV // 2
LAST_RUN = 1024 - RUN
SEQ_Z = 4
SEQ_Y = 8
ROWS = NEW_DEV * HPK
INFO = 16
V_AT = CACHE_DEV
NEW_K_AT = 2 * CACHE_DEV
NEW_V_AT = NEW_K_AT + NEW_DEV
INFO_AT = NEW_V_AT + NEW_DEV
KV_ROWS = INFO_AT + INFO
SCALE = math.log2(math.e) / math.sqrt(DH)
HIDDEN = -1e30
CHUNK = 512
PIECE = 64
UNROLL = 4
CEILING = 2.0**60

F32 = jnp.float32
BF16 = jnp.bfloat16


def iota(shape, dim):
    return lax.broadcasted_iota(jnp.int32, shape, dim)


def pack_kv_kernel(len_hbm, pos_hbm, kv_ref, new_ref, kv_out, cache_len, new_pos, sems):
    copies = [
        pltpu.make_async_copy(len_hbm, cache_len, sems.at[0]),
        pltpu.make_async_copy(pos_hbm, new_pos, sems.at[1]),
    ]
    for copy in copies:
        copy.start()
    kv_out[NEW_K_AT:NEW_V_AT] = new_ref[0]
    kv_out[NEW_V_AT:INFO_AT] = new_ref[1]
    first_key = kv_ref[0, 0:16, :].astype(F32)[0:1]
    for copy in copies:
        copy.wait()
    info_row = iota((INFO, DH), 0)
    info = jnp.full((INFO, DH), (new_pos[0] // RUN).astype(F32), F32)
    kept = []
    for b in range(4):
        length = cache_len[b]
        info = jnp.where(info_row == b, length.astype(F32), info)
        rows = slice(b * BLOCK, (b + 1) * BLOCK)
        live = iota((BLOCK, DH), 0) < length
        kept.append(jnp.where(live, kv_ref[0, rows, :].astype(F32), first_key))
        values = kv_ref[1, rows, :].astype(F32)
        kv_out[V_AT + b * BLOCK : V_AT + (b + 1) * BLOCK] = jnp.where(live, values, 0.0).astype(BF16)
    keys = jnp.concatenate(kept, axis=0)
    for t in range(CACHE_DEV // DH):
        rows = slice(t * DH, (t + 1) * DH)
        kv_out[rows] = jnp.transpose(keys[rows]).astype(BF16)
    kv_out[INFO_AT:KV_ROWS] = info.astype(BF16)


def pack_kv(kv_cache, new_kv, cache_len, new_pos):
    vmem = pl.BlockSpec(memory_space=pltpu.VMEM)
    hbm = pl.BlockSpec(memory_space=pl.ANY)
    return pl.pallas_call(
        pack_kv_kernel,
        out_shape=jax.ShapeDtypeStruct((KV_ROWS, DH), BF16),
        in_specs=[hbm, hbm, vmem, vmem],
        out_specs=vmem,
        scratch_shapes=[
            pltpu.SMEM(cache_len.shape, jnp.int32),
            pltpu.SMEM(new_pos.shape, jnp.int32),
            pltpu.SemaphoreType.DMA((2,)),
        ],
        compiler_params=pltpu.CompilerParams(vmem_limit_bytes=16 << 20),
        name="pack_kv",
    )(cache_len, new_pos, jnp.transpose(kv_cache, (1, 0, 2)), jnp.transpose(new_kv, (1, 0, 2)))


def pack_q_kernel(q_ref, kv_ref, out_ref):
    for h in range(HPK):
        out_ref[h * NEW_DEV : (h + 1) * NEW_DEV] = q_ref[:, h * DH : (h + 1) * DH]
    run = kv_ref[INFO_AT:KV_ROWS].astype(F32)[4:5]
    out_ref[ROWS : ROWS + INFO] = jnp.broadcast_to(run, (INFO, DH)).astype(BF16)


def pack_q(queries, own_kv):
    vmem = pl.BlockSpec(memory_space=pltpu.VMEM)
    return pl.pallas_call(
        pack_q_kernel,
        out_shape=jax.ShapeDtypeStruct((ROWS + INFO, DH), BF16),
        in_specs=[vmem, vmem],
        out_specs=vmem,
        compiler_params=pltpu.CompilerParams(vmem_limit_bytes=16 << 20),
        name="pack_q",
    )(queries, own_kv)


def stage_kernel(nq, g, spans, last, *refs):
    first = not spans
    refs = list(refs)
    take = lambda n: [refs.pop(0) for _ in range(n)]
    q_refs, kv_refs = take(nq), take(g)
    states = [(0, nq * ROWS, None, None)]
    if not first:
        states, begin = [], 0
        for span in spans:
            states.append((begin, span, *take(2)))
            begin += span
    if last:
        outs = take(nq)
    else:
        acc_out, top_out = take(2)
    qs, kk, vv, bias = take(4)
    if last:
        mix, lse = take(2)
    new_pad = bias.shape[1]

    lane = iota((NEW_DEV, new_pad), 1)
    within = lane % NEW_DEV
    token = iota((NEW_DEV, new_pad), 0)
    base = jnp.zeros((1, new_pad), F32)
    new_row = g * CACHE_DEV
    fresh_keys = []
    for j, kv_ref in enumerate(kv_refs):
        info = kv_ref[INFO_AT:KV_ROWS].astype(F32)
        wide = jnp.concatenate([info] * (new_pad // DH), axis=1)
        base = jnp.where(lane[0:1] // NEW_DEV == j, wide[4:5] * RUN, base)
        for t in range(CACHE_DEV // DH):
            at = j * CACHE_DEV + t * DH
            kk[:, at : at + DH] = kv_ref[t * DH : (t + 1) * DH]
        for b in range(4):
            dst = slice(j * CACHE_DEV + b * BLOCK, j * CACHE_DEV + (b + 1) * BLOCK)
            vv[dst, 0:DH] = kv_ref[V_AT + b * BLOCK : V_AT + (b + 1) * BLOCK]
            live = iota((BLOCK, DH), 0).astype(F32) < info[b : b + 1]
            vv[dst, DH:] = jnp.where(live, 1.0, 0.0).astype(BF16)
        fresh_keys.append(kv_ref[NEW_K_AT:NEW_V_AT].astype(F32))
        dst = slice(new_row + j * NEW_DEV, new_row + (j + 1) * NEW_DEV)
        vv[dst, 0:DH] = kv_ref[NEW_V_AT:INFO_AT]
        vv[dst, DH:] = jnp.ones((NEW_DEV, DH), BF16)
    rest = new_pad - g * NEW_DEV
    if rest:
        fresh_keys.append(jnp.zeros((rest, DH), F32))
        vv[new_row + g * NEW_DEV : new_row + new_pad, :] = jnp.zeros((rest, 2 * DH), BF16)
    fresh_keys = jnp.concatenate(fresh_keys, axis=0)
    for t in range(new_pad // DH):
        turned = jnp.transpose(fresh_keys[t * DH : (t + 1) * DH])
        kk[:, new_row + t * DH : new_row + (t + 1) * DH] = turned.astype(BF16)
    within_f = within.astype(F32)
    key_pos = jnp.where(within < RUN, base + within_f, LAST_RUN - RUN - base + within_f)
    token_f = token.astype(F32)
    for i, q_ref in enumerate(q_refs):
        qs[i * ROWS : (i + 1) * ROWS] = q_ref[0:ROWS]
        run = q_ref[ROWS : ROWS + INFO].astype(F32)[0:1] * RUN
        start = jnp.concatenate([run] * (new_pad // DH), axis=1)
        pos = jnp.where(token < RUN, start + token_f, LAST_RUN - RUN - start + token_f)
        seen = (key_pos <= pos) & (lane < g * NEW_DEV)
        bias[i * NEW_DEV : (i + 1) * NEW_DEV] = jnp.where(seen, 0.0, HIDDEN)

    def new_scores(q, at, count):
        block = pl.multiple_of((at // ROWS) * NEW_DEV, NEW_DEV)
        mask = bias[pl.ds(block, NEW_DEV), :]
        fresh = jnp.dot(q, kk[:, new_row : new_row + new_pad], preferred_element_type=F32)
        fresh = fresh.reshape(count // NEW_DEV, NEW_DEV, new_pad) + mask[None]
        return fresh.reshape(count, new_pad)

    def cached_scores(q, j):
        keys = kk[:, j * CACHE_DEV : (j + 1) * CACHE_DEV]
        return jnp.dot(q, keys, preferred_element_type=F32)

    def weigh(s, top):
        return jnp.exp2((s - top) * SCALE).astype(BF16)

    def keep_result(rows, count, total, top):
        if last:
            acc, length = total[:, 0:DH], total[:, DH:]
            mix[rows, :] = (acc / length).astype(BF16)
            lse[rows, :] = top * SCALE + jnp.log2(length)
        else:
            acc_out[rows, :] = total
            top_out[rows, :] = jnp.broadcast_to(top, (count, DH))

    def piece(at, begin, acc_in, top_in):
        rows, past = pl.ds(at, PIECE), pl.ds(at - begin, PIECE)
        q = qs[rows, :]
        fresh = new_scores(q, at, PIECE)
        scores = [cached_scores(q, j) for j in range(g)]
        top = jnp.max(fresh, axis=1, keepdims=True)
        for s in scores:
            top = jnp.maximum(top, jnp.max(s, axis=1, keepdims=True))
        if not first:
            old = top_in[past, :]
            top = jnp.maximum(top, old[:, 0:1])
        total = jnp.dot(weigh(fresh, top), vv[new_row:, :], preferred_element_type=F32)
        for j, s in enumerate(scores):
            values = vv[j * CACHE_DEV : (j + 1) * CACHE_DEV, :]
            total += jnp.dot(weigh(s, top), values, preferred_element_type=F32)
        if not first:
            keep = jnp.exp2((old - top) * SCALE)
            total += acc_in[past, :] * jnp.concatenate([keep, keep], axis=1)
        keep_result(rows, PIECE, total, top)

    def chunk(begin, acc_in, top_in, c, carry):
        at = pl.multiple_of(begin + c * CHUNK, CHUNK)
        rows, past = pl.ds(at, CHUNK), pl.ds(pl.multiple_of(c * CHUNK, CHUNK), CHUNK)
        q = qs[rows, :]
        if first:
            lead = jnp.dot(q, kk[:, 0:DH], preferred_element_type=F32)
            top = jnp.max(lead, axis=1, keepdims=True)
        else:
            top = top_in[past, 0:1]
        fresh = weigh(new_scores(q, at, CHUNK), top)
        total = jnp.dot(fresh, vv[new_row:, :], preferred_element_type=F32)
        for j in range(g):
            values = vv[j * CACHE_DEV : (j + 1) * CACHE_DEV, :]
            total += jnp.dot(weigh(cached_scores(q, j), top), values, preferred_element_type=F32)
        over = jnp.where(total[:, DH:] < CEILING, 0.0, 1.0).reshape(CHUNK // 8, 8, DH)
        carry = jnp.maximum(carry, jnp.max(over, axis=0))
        if not first:
            total += acc_in[past, :]
        keep_result(rows, CHUNK, total, top)

        return carry

    worst = jnp.zeros((8, DH), F32)
    for begin, span, acc_in, top_in in states:
        step = functools.partial(chunk, begin, acc_in, top_in)
        count = span // CHUNK
        worst = lax.fori_loop(0, count, step, worst, unroll=UNROLL if count % UNROLL == 0 else 1)

    @pl.when(jnp.max(worst) > 0.0)
    def _():
        for begin, span, acc_in, top_in in states:

            def careful(k, carry):
                piece(pl.multiple_of(begin + k * PIECE, PIECE), begin, acc_in, top_in)
                return carry

            lax.fori_loop(0, span // PIECE, careful, 0)

    if last:
        row = iota((INFO, DH), 0)
        for i in range(nq):
            outs[i][0:ROWS] = mix[i * ROWS : (i + 1) * ROWS]
            tile = jnp.zeros((INFO, DH), F32)
            for part in range(ROWS // DH):
                at = i * ROWS + part * DH
                turned = jnp.transpose(lse[at : at + DH, :])[0:INFO]
                high = turned.astype(BF16).astype(F32)
                middle = (turned - high).astype(BF16).astype(F32)
                low = turned - high - middle
                tile = jnp.where(row == part, high, tile)
                tile = jnp.where(row == 4 + part, middle, tile)
                tile = jnp.where(row == 8 + part, low, tile)
            outs[i][ROWS : ROWS + INFO] = tile.astype(BF16)


def stage(qs, kvs, states, last, name):
    nq, g = len(qs), len(kvs)
    spans = tuple(acc.shape[0] for acc, _ in states)
    new_pad = -(-g * NEW_DEV // DH) * DH
    rows, keys = nq * ROWS, g * CACHE_DEV + new_pad
    vmem = pl.BlockSpec(memory_space=pltpu.VMEM)
    if last:
        out_shape = tuple(jax.ShapeDtypeStruct((ROWS + INFO, DH), BF16) for _ in range(nq))
    else:
        out_shape = (
            jax.ShapeDtypeStruct((rows, 2 * DH), F32),
            jax.ShapeDtypeStruct((rows, DH), F32),
        )
    scratch = [
        pltpu.VMEM((rows, DH), BF16),
        pltpu.VMEM((DH, keys), BF16),
        pltpu.VMEM((keys, 2 * DH), BF16),
        pltpu.VMEM((nq * NEW_DEV, new_pad), F32),
    ]
    if last:
        scratch += [pltpu.VMEM((rows, DH), BF16), pltpu.VMEM((rows, DH), F32)]
    operands = [*qs, *kvs, *(x for state in states for x in state)]
    return pl.pallas_call(
        functools.partial(stage_kernel, nq, g, spans, last),
        out_shape=out_shape,
        in_specs=[vmem] * len(operands),
        out_specs=(vmem,) * len(out_shape),
        scratch_shapes=scratch,
        compiler_params=pltpu.CompilerParams(vmem_limit_bytes=32 << 20),
        cost_estimate=pl.CostEstimate(
            flops=8 * rows * keys * DH, bytes_accessed=4 << 20, transcendentals=rows * keys
        ),
        name=name,
    )(*operands)


def combine_kernel(*refs):
    parts, out_ref = refs[:-1], refs[-1]
    n = len(parts)
    tiles = [parts[i][ROWS : ROWS + INFO].astype(F32) for i in range(n)]
    for c in range(ROWS // DH):
        logs = []
        for tile in tiles:
            line = tile[c : c + 1] + tile[4 + c : 5 + c] + tile[8 + c : 9 + c]
            logs.append(jnp.transpose(jnp.broadcast_to(line, (DH, DH))))
        peak = functools.reduce(jnp.maximum, logs)
        shares = [jnp.exp2(x - peak) for x in logs]
        total = functools.reduce(jnp.add, shares)
        summed = functools.reduce(
            jnp.add,
            [w * parts[i][c * DH : (c + 1) * DH].astype(F32) for i, w in enumerate(shares)],
        )
        result = (summed / total).astype(BF16)
        for k in range(DH // NEW_DEV):
            h = c * (DH // NEW_DEV) + k
            out_ref[:, h * DH : (h + 1) * DH] = result[k * NEW_DEV : (k + 1) * NEW_DEV]


def combine(parts):
    vmem = pl.BlockSpec(memory_space=pltpu.VMEM)
    return pl.pallas_call(
        combine_kernel,
        out_shape=jax.ShapeDtypeStruct((NEW_DEV, HPK * DH), BF16),
        in_specs=[vmem] * len(parts),
        out_specs=vmem,
        compiler_params=pltpu.CompilerParams(vmem_limit_bytes=16 << 20),
        name="combine",
    )(*parts)


def shift_y(x, d):
    pairs = [
        (z * SEQ_Y + y, z * SEQ_Y + (y + d) % SEQ_Y) for z in range(SEQ_Z) for y in range(SEQ_Y)
    ]
    return lax.ppermute(x, "seq", pairs)


def shift_z(x, d):
    pairs = [
        (z * SEQ_Y + y, (z + d) % SEQ_Z * SEQ_Y + y) for z in range(SEQ_Z) for y in range(SEQ_Y)
    ]
    return lax.ppermute(x, "seq", pairs)


def body(queries, kv_cache, new_kv, cache_len, new_pos):
    own_kv = pack_kv(kv_cache, new_kv, cache_len, new_pos)
    own_q = pack_q(queries, own_kv)
    down1 = shift_y(own_kv, -1)
    same_kv, own_q = lax.optimization_barrier((own_kv, own_q))
    up1 = shift_y(same_kv, 1)
    offsets = (1, -1, 2)
    q1, q2, q3 = [shift_z(own_q, d) for d in offsets]
    up2, down2 = shift_y(up1, 1), shift_y(down1, -1)
    up3, down3 = shift_y(up2, 1), shift_y(down2, -1)
    qs = [own_q, q1, q2, q3]
    state = stage(qs, [own_kv, up1, down1], [], False, "reach1")
    up3, state = lax.optimization_barrier((up3, state))
    far = shift_y(up3, 1)
    state = stage(qs, [up2, down2, up3, down3], [state], False, "reach3")
    far, state = lax.optimization_barrier((far, state))
    parts = stage(qs, [far], [state], True, "reach4")
    back = [parts[0], shift_z(parts[3], -2), shift_z(parts[1], -1), shift_z(parts[2], 1)]
    return combine(back)


def solution(mesh):
    return jax.shard_map(
        body,
        mesh=mesh,
        in_specs=(
            P(("batch", "seq"), "head"),
            P(("batch", "seq"), None, "head"),
            P(("batch", "seq"), None, "head"),
            P(("batch", "seq")),
            P(("batch", "seq")),
        ),
        out_specs=P(("batch", "seq"), "head"),
        check_vma=False,
    )
```

```python
import functools
import math

import jax
import jax.numpy as jnp
from jax import lax
from jax.experimental import pallas as pl
from jax.experimental.pallas import tpu as pltpu
from jax.sharding import PartitionSpec as P

HPK = 16
DH = 128
NEW_DEV = 32
CACHE_DEV = 768
BLOCK = CACHE_DEV // 4
RUN = NEW_DEV // 2
LAST_RUN = 1024 - RUN
SEQ_Z = 4
SEQ_Y = 8
ROWS = NEW_DEV * HPK
INFO = 16
V_AT = CACHE_DEV
NEW_K_AT = 2 * CACHE_DEV
NEW_V_AT = NEW_K_AT + NEW_DEV
INFO_AT = NEW_V_AT + NEW_DEV
KV_ROWS = INFO_AT + INFO
SCALE = math.log2(math.e) / math.sqrt(DH)
HIDDEN = -1e30
CHUNK = 512
PIECE = 64
UNROLL = 4
CEILING = 2.0**60

F32 = jnp.float32
BF16 = jnp.bfloat16


def iota(shape, dim):
    return lax.broadcasted_iota(jnp.int32, shape, dim)


def pack_kv_kernel(len_hbm, pos_hbm, kv_ref, new_ref, kv_out, cache_len, new_pos, sems):
    copies = [
        pltpu.make_async_copy(len_hbm, cache_len, sems.at[0]),
        pltpu.make_async_copy(pos_hbm, new_pos, sems.at[1]),
    ]
    for copy in copies:
        copy.start()
    kv_out[NEW_K_AT:NEW_V_AT] = new_ref[0]
    kv_out[NEW_V_AT:INFO_AT] = new_ref[1]
    first_key = kv_ref[0, 0:16, :].astype(F32)[0:1]
    for copy in copies:
        copy.wait()
    info_row = iota((INFO, DH), 0)
    info = jnp.full((INFO, DH), (new_pos[0] // RUN).astype(F32), F32)
    kept = []
    for b in range(4):
        length = cache_len[b]
        info = jnp.where(info_row == b, length.astype(F32), info)
        rows = slice(b * BLOCK, (b + 1) * BLOCK)
        live = iota((BLOCK, DH), 0) < length
        kept.append(jnp.where(live, kv_ref[0, rows, :].astype(F32), first_key))
        values = kv_ref[1, rows, :].astype(F32)
        kv_out[V_AT + b * BLOCK : V_AT + (b + 1) * BLOCK] = jnp.where(live, values, 0.0).astype(BF16)
    keys = jnp.concatenate(kept, axis=0)
    for t in range(CACHE_DEV // DH):
        rows = slice(t * DH, (t + 1) * DH)
        kv_out[rows] = jnp.transpose(keys[rows]).astype(BF16)
    kv_out[INFO_AT:KV_ROWS] = info.astype(BF16)


def pack_kv(kv_cache, new_kv, cache_len, new_pos):
    vmem = pl.BlockSpec(memory_space=pltpu.VMEM)
    hbm = pl.BlockSpec(memory_space=pl.ANY)
    return pl.pallas_call(
        pack_kv_kernel,
        out_shape=jax.ShapeDtypeStruct((KV_ROWS, DH), BF16),
        in_specs=[hbm, hbm, vmem, vmem],
        out_specs=vmem,
        scratch_shapes=[
            pltpu.SMEM(cache_len.shape, jnp.int32),
            pltpu.SMEM(new_pos.shape, jnp.int32),
            pltpu.SemaphoreType.DMA((2,)),
        ],
        compiler_params=pltpu.CompilerParams(vmem_limit_bytes=16 << 20),
        name="pack_kv",
    )(cache_len, new_pos, jnp.transpose(kv_cache, (1, 0, 2)), jnp.transpose(new_kv, (1, 0, 2)))


def pack_q_kernel(q_ref, kv_ref, out_ref):
    for h in range(HPK):
        out_ref[h * NEW_DEV : (h + 1) * NEW_DEV] = q_ref[:, h * DH : (h + 1) * DH]
    run = kv_ref[INFO_AT:KV_ROWS].astype(F32)[4:5]
    out_ref[ROWS : ROWS + INFO] = jnp.broadcast_to(run, (INFO, DH)).astype(BF16)


def pack_q(queries, own_kv):
    vmem = pl.BlockSpec(memory_space=pltpu.VMEM)
    return pl.pallas_call(
        pack_q_kernel,
        out_shape=jax.ShapeDtypeStruct((ROWS + INFO, DH), BF16),
        in_specs=[vmem, vmem],
        out_specs=vmem,
        compiler_params=pltpu.CompilerParams(vmem_limit_bytes=16 << 20),
        name="pack_q",
    )(queries, own_kv)


def stage_kernel(nq, g, spans, last, *refs):
    first = not spans
    refs = list(refs)
    take = lambda n: [refs.pop(0) for _ in range(n)]
    q_refs, kv_refs = take(nq), take(g)
    states = [(0, nq * ROWS, None, None)]
    if not first:
        states, begin = [], 0
        for span in spans:
            states.append((begin, span, *take(2)))
            begin += span
    if last:
        outs = take(nq)
    else:
        acc_out, top_out = take(2)
    qs, kk, vv, bias = take(4)
    if last:
        mix, lse = take(2)
    new_pad = bias.shape[1]

    lane = iota((NEW_DEV, new_pad), 1)
    within = lane % NEW_DEV
    token = iota((NEW_DEV, new_pad), 0)
    base = jnp.zeros((1, new_pad), F32)
    new_row = g * CACHE_DEV
    fresh_keys = []
    for j, kv_ref in enumerate(kv_refs):
        info = kv_ref[INFO_AT:KV_ROWS].astype(F32)
        wide = jnp.concatenate([info] * (new_pad // DH), axis=1)
        base = jnp.where(lane[0:1] // NEW_DEV == j, wide[4:5] * RUN, base)
        for t in range(CACHE_DEV // DH):
            at = j * CACHE_DEV + t * DH
            kk[:, at : at + DH] = kv_ref[t * DH : (t + 1) * DH]
        for b in range(4):
            dst = slice(j * CACHE_DEV + b * BLOCK, j * CACHE_DEV + (b + 1) * BLOCK)
            vv[dst, 0:DH] = kv_ref[V_AT + b * BLOCK : V_AT + (b + 1) * BLOCK]
            live = iota((BLOCK, DH), 0).astype(F32) < info[b : b + 1]
            vv[dst, DH:] = jnp.where(live, 1.0, 0.0).astype(BF16)
        fresh_keys.append(kv_ref[NEW_K_AT:NEW_V_AT].astype(F32))
        dst = slice(new_row + j * NEW_DEV, new_row + (j + 1) * NEW_DEV)
        vv[dst, 0:DH] = kv_ref[NEW_V_AT:INFO_AT]
        vv[dst, DH:] = jnp.ones((NEW_DEV, DH), BF16)
    rest = new_pad - g * NEW_DEV
    if rest:
        fresh_keys.append(jnp.zeros((rest, DH), F32))
        vv[new_row + g * NEW_DEV : new_row + new_pad, :] = jnp.zeros((rest, 2 * DH), BF16)
    fresh_keys = jnp.concatenate(fresh_keys, axis=0)
    for t in range(new_pad // DH):
        turned = jnp.transpose(fresh_keys[t * DH : (t + 1) * DH])
        kk[:, new_row + t * DH : new_row + (t + 1) * DH] = turned.astype(BF16)
    within_f = within.astype(F32)
    key_pos = jnp.where(within < RUN, base + within_f, LAST_RUN - RUN - base + within_f)
    token_f = token.astype(F32)
    for i, q_ref in enumerate(q_refs):
        qs[i * ROWS : (i + 1) * ROWS] = q_ref[0:ROWS]
        run = q_ref[ROWS : ROWS + INFO].astype(F32)[0:1] * RUN
        start = jnp.concatenate([run] * (new_pad // DH), axis=1)
        pos = jnp.where(token < RUN, start + token_f, LAST_RUN - RUN - start + token_f)
        seen = (key_pos <= pos) & (lane < g * NEW_DEV)
        bias[i * NEW_DEV : (i + 1) * NEW_DEV] = jnp.where(seen, 0.0, HIDDEN)

    def new_scores(q, at, count):
        block = pl.multiple_of((at // ROWS) * NEW_DEV, NEW_DEV)
        mask = bias[pl.ds(block, NEW_DEV), :]
        fresh = jnp.dot(q, kk[:, new_row : new_row + new_pad], preferred_element_type=F32)
        fresh = fresh.reshape(count // NEW_DEV, NEW_DEV, new_pad) + mask[None]
        return fresh.reshape(count, new_pad)

    def cached_scores(q, j):
        keys = kk[:, j * CACHE_DEV : (j + 1) * CACHE_DEV]
        return jnp.dot(q, keys, preferred_element_type=F32)

    def weigh(s, top):
        return jnp.exp2((s - top) * SCALE).astype(BF16)

    def keep_result(rows, count, total, top):
        if last:
            acc, length = total[:, 0:DH], total[:, DH:]
            mix[rows, :] = (acc / length).astype(BF16)
            lse[rows, :] = top * SCALE + jnp.log2(length)
        else:
            acc_out[rows, :] = total
            top_out[rows, :] = jnp.broadcast_to(top, (count, DH))

    def piece(at, begin, acc_in, top_in):
        rows, past = pl.ds(at, PIECE), pl.ds(at - begin, PIECE)
        q = qs[rows, :]
        fresh = new_scores(q, at, PIECE)
        scores = [cached_scores(q, j) for j in range(g)]
        top = jnp.max(fresh, axis=1, keepdims=True)
        for s in scores:
            top = jnp.maximum(top, jnp.max(s, axis=1, keepdims=True))
        if not first:
            old = top_in[past, :]
            top = jnp.maximum(top, old[:, 0:1])
        total = jnp.dot(weigh(fresh, top), vv[new_row:, :], preferred_element_type=F32)
        for j, s in enumerate(scores):
            values = vv[j * CACHE_DEV : (j + 1) * CACHE_DEV, :]
            total += jnp.dot(weigh(s, top), values, preferred_element_type=F32)
        if not first:
            keep = jnp.exp2((old - top) * SCALE)
            total += acc_in[past, :] * jnp.concatenate([keep, keep], axis=1)
        keep_result(rows, PIECE, total, top)

    def chunk(begin, acc_in, top_in, c, carry):
        at = pl.multiple_of(begin + c * CHUNK, CHUNK)
        rows, past = pl.ds(at, CHUNK), pl.ds(pl.multiple_of(c * CHUNK, CHUNK), CHUNK)
        q = qs[rows, :]
        if first:
            lead = jnp.dot(q, kk[:, 0:DH], preferred_element_type=F32)
            top = jnp.max(lead, axis=1, keepdims=True)
        else:
            top = top_in[past, 0:1]
        fresh = weigh(new_scores(q, at, CHUNK), top)
        total = jnp.dot(fresh, vv[new_row:, :], preferred_element_type=F32)
        for j in range(g):
            values = vv[j * CACHE_DEV : (j + 1) * CACHE_DEV, :]
            total += jnp.dot(weigh(cached_scores(q, j), top), values, preferred_element_type=F32)
        over = jnp.where(total[:, DH:] < CEILING, 0.0, 1.0).reshape(CHUNK // 8, 8, DH)
        carry = jnp.maximum(carry, jnp.max(over, axis=0))
        if not first:
            total += acc_in[past, :]
        keep_result(rows, CHUNK, total, top)

        return carry

    worst = jnp.zeros((8, DH), F32)
    for begin, span, acc_in, top_in in states:
        step = functools.partial(chunk, begin, acc_in, top_in)
        count = span // CHUNK
        worst = lax.fori_loop(0, count, step, worst, unroll=UNROLL if count % UNROLL == 0 else 1)

    @pl.when(jnp.max(worst) > 0.0)
    def _():
        for begin, span, acc_in, top_in in states:

            def careful(k, carry):
                piece(pl.multiple_of(begin + k * PIECE, PIECE), begin, acc_in, top_in)
                return carry

            lax.fori_loop(0, span // PIECE, careful, 0)

    if last:
        row = iota((INFO, DH), 0)
        for i in range(nq):
            outs[i][0:ROWS] = mix[i * ROWS : (i + 1) * ROWS]
            tile = jnp.zeros((INFO, DH), F32)
            for part in range(ROWS // DH):
                at = i * ROWS + part * DH
                turned = jnp.transpose(lse[at : at + DH, :])[0:INFO]
                high = turned.astype(BF16).astype(F32)
                middle = (turned - high).astype(BF16).astype(F32)
                low = turned - high - middle
                tile = jnp.where(row == part, high, tile)
                tile = jnp.where(row == 4 + part, middle, tile)
                tile = jnp.where(row == 8 + part, low, tile)
            outs[i][ROWS : ROWS + INFO] = tile.astype(BF16)


def stage(qs, kvs, states, last, name):
    nq, g = len(qs), len(kvs)
    spans = tuple(acc.shape[0] for acc, _ in states)
    new_pad = -(-g * NEW_DEV // DH) * DH
    rows, keys = nq * ROWS, g * CACHE_DEV + new_pad
    vmem = pl.BlockSpec(memory_space=pltpu.VMEM)
    if last:
        out_shape = tuple(jax.ShapeDtypeStruct((ROWS + INFO, DH), BF16) for _ in range(nq))
    else:
        out_shape = (
            jax.ShapeDtypeStruct((rows, 2 * DH), F32),
            jax.ShapeDtypeStruct((rows, DH), F32),
        )
    scratch = [
        pltpu.VMEM((rows, DH), BF16),
        pltpu.VMEM((DH, keys), BF16),
        pltpu.VMEM((keys, 2 * DH), BF16),
        pltpu.VMEM((nq * NEW_DEV, new_pad), F32),
    ]
    if last:
        scratch += [pltpu.VMEM((rows, DH), BF16), pltpu.VMEM((rows, DH), F32)]
    operands = [*qs, *kvs, *(x for state in states for x in state)]
    return pl.pallas_call(
        functools.partial(stage_kernel, nq, g, spans, last),
        out_shape=out_shape,
        in_specs=[vmem] * len(operands),
        out_specs=(vmem,) * len(out_shape),
        scratch_shapes=scratch,
        compiler_params=pltpu.CompilerParams(vmem_limit_bytes=32 << 20),
        cost_estimate=pl.CostEstimate(
            flops=8 * rows * keys * DH, bytes_accessed=4 << 20, transcendentals=rows * keys
        ),
        name=name,
    )(*operands)


def combine_kernel(*refs):
    parts, out_ref = refs[:-1], refs[-1]
    n = len(parts)
    tiles = [parts[i][ROWS : ROWS + INFO].astype(F32) for i in range(n)]
    for c in range(ROWS // DH):
        logs = []
        for tile in tiles:
            line = tile[c : c + 1] + tile[4 + c : 5 + c] + tile[8 + c : 9 + c]
            logs.append(jnp.transpose(jnp.broadcast_to(line, (DH, DH))))
        peak = functools.reduce(jnp.maximum, logs)
        shares = [jnp.exp2(x - peak) for x in logs]
        total = functools.reduce(jnp.add, shares)
        summed = functools.reduce(
            jnp.add,
            [w * parts[i][c * DH : (c + 1) * DH].astype(F32) for i, w in enumerate(shares)],
        )
        result = (summed / total).astype(BF16)
        for k in range(DH // NEW_DEV):
            h = c * (DH // NEW_DEV) + k
            out_ref[:, h * DH : (h + 1) * DH] = result[k * NEW_DEV : (k + 1) * NEW_DEV]


def combine(parts):
    vmem = pl.BlockSpec(memory_space=pltpu.VMEM)
    return pl.pallas_call(
        combine_kernel,
        out_shape=jax.ShapeDtypeStruct((NEW_DEV, HPK * DH), BF16),
        in_specs=[vmem] * len(parts),
        out_specs=vmem,
        compiler_params=pltpu.CompilerParams(vmem_limit_bytes=16 << 20),
        name="combine",
    )(*parts)


def shift_y(x, d):
    pairs = [
        (z * SEQ_Y + y, z * SEQ_Y + (y + d) % SEQ_Y) for z in range(SEQ_Z) for y in range(SEQ_Y)
    ]
    return lax.ppermute(x, "seq", pairs)


def shift_z(x, d):
    pairs = [
        (z * SEQ_Y + y, (z + d) % SEQ_Z * SEQ_Y + y) for z in range(SEQ_Z) for y in range(SEQ_Y)
    ]
    return lax.ppermute(x, "seq", pairs)


def body(queries, kv_cache, new_kv, cache_len, new_pos):
    own_kv = pack_kv(kv_cache, new_kv, cache_len, new_pos)
    own_q = pack_q(queries, own_kv)
    down1 = shift_y(own_kv, -1)
    up1 = shift_y(own_kv, 1)
    offsets = (1, -1, 2)
    q1, q2, q3 = [shift_z(own_q, d) for d in offsets]
    up2, down2 = shift_y(up1, 1), shift_y(down1, -1)
    up3, down3 = shift_y(up2, 1), shift_y(down2, -1)
    qs = [own_q, q1, q2, q3]
    state = stage(qs, [own_kv, up1, down1], [], False, "reach1")
    up3, state = lax.optimization_barrier((up3, state))
    far = shift_y(up3, 1)
    state = stage(qs, [up2, down2, up3, down3], [state], False, "reach3")
    far, state = lax.optimization_barrier((far, state))
    parts = stage(qs, [far], [state], True, "reach4")
    back = [parts[0], shift_z(parts[3], -2), shift_z(parts[1], -1), shift_z(parts[2], 1)]
    return combine(back)


def solution(mesh):
    return jax.shard_map(
        body,
        mesh=mesh,
        in_specs=(
            P(("batch", "seq"), "head"),
            P(("batch", "seq"), None, "head"),
            P(("batch", "seq"), None, "head"),
            P(("batch", "seq")),
            P(("batch", "seq")),
        ),
        out_specs=P(("batch", "seq"), "head"),
        check_vma=False,
    )
```
